512 devices in a mesh: dp: 32 (over z, core), shard: 16 (over x, y).
Axes of the slice: x: 4, y: 4, z: 16, core: 2. Of those that a mesh axis runs over, the one named last changes fastest.
Arguments:
- grads: bfloat16 [32, 1024, 7168], P('dp', 'shard'), may hold values from -6 to 6
- errors: float32 [32, 1024, 7168], P('dp', 'shard'), may hold values from -4 to 4
- q_prev: float32 [7168, 32], P('shard'), may hold values from -6 to 6
Outputs:
- new_errors: float32 [32, 1024, 7168], P('dp', 'shard')
- q_new: float32 [7168, 32], P('shard')
The draws below stay inside these ranges and needn't reach their ends.
All inputs are finite; a program needn't handle non-finite values.
Results may differ from the reference program's by a relative error of at most 0.0003.
Values sent between devices are 32-bit elements; how exact they have to be, the bound alone decides.
No kernel may reach another device: no remote copies, remote signals or barrier semaphores. Data moves between devices by JAX's collectives and lax.ppermute only.
A program may use at most 64 MiB of HBM per device.

```python
import jax
import jax.numpy as jnp
from jax import lax

D = 7168
RANK = 32
ROWS = 1024
N_DP = 32


def block_levels(rng, extent, pieces, smallest, largest):
    loudness, own = 1.0, jax.random.fold_in(rng, 6)
    for axis_at, parts in pieces:
        heights = jnp.exp(jax.random.uniform(jax.random.fold_in(own, axis_at), (parts,), jnp.float32, smallest / len(pieces), largest / len(pieces)))
        loudness = loudness * jnp.repeat(heights, extent[axis_at] // parts).reshape([-1 if axis == axis_at else 1 for axis in range(len(extent))])
    return loudness


def gaussian(rng, shape, width, reach, split=(), dtype=jnp.bfloat16):
    values = jax.random.normal(rng, shape, jnp.float32) * width
    if len(split) > 0:
        values = block_levels(rng, shape, split, -0.22, 0.18) * values
    return jnp.clip(values, min=-reach, max=reach).astype(dtype)


def setup_inputs(seed: int = 0) -> dict:
    streams_of = jax.random.split(jax.random.key(seed), 4)
    grads = gaussian(streams_of[0], (N_DP, ROWS, D), 1.0, 6.0, ((0, 32), (1, 16)))
    errors = gaussian(streams_of[1], (N_DP, ROWS, D), 0.5, 4.0, ((0, 32), (1, 16)), jnp.float32)
    q_prev = gaussian(streams_of[2], (D, RANK), 1.0, 6.0, ((0, 16),), jnp.float32)
    return {"grads": grads, "errors": errors, "q_prev": q_prev}


def reference(grads, errors, q_prev):
    high = lax.Precision.HIGHEST
    merged = grads.astype(jnp.float32) + errors
    left = jnp.einsum('krd,dc->rc', merged, q_prev, precision=high) / N_DP
    gram = jnp.dot(left.T, left, precision=high)
    lower = jnp.linalg.cholesky(gram)
    p_hat = jax.scipy.linalg.solve_triangular(lower, left.T, lower=True).T
    right = jnp.einsum('krd,rc->dc', merged, p_hat, precision=high) / N_DP
    approx = jnp.dot(p_hat, right.T, precision=high)
    return (merged - approx[None], right)
```

```python
import jax
import jax.numpy as jnp
from jax import lax
from jax.sharding import Mesh, PartitionSpec as P

HIGH = lax.Precision.HIGHEST
PLANE = ("x", "y")


def to_all(block, peers, axis):
    return lax.all_to_all(jnp.broadcast_to(block, (peers, *block.shape)), axis, 0, 0)


def per_device(grads, errors, q_prev):
    merged = grads[0].astype(jnp.float32) + errors[0]
    rows, width = merged.shape
    share, rank = q_prev.shape
    planes, chips = lax.axis_size("z"), lax.axis_size(PLANE)
    replicas = 2 * planes
    half = rank // 2
    core = lax.axis_index("core")
    here = lax.axis_index(PLANE)

    other = lax.ppermute(merged, "core", [(0, 1), (1, 0)])
    own_q = lax.dynamic_slice_in_dim(q_prev.T, core * half, half, 0)
    all_q = to_all(own_q, chips, PLANE)
    all_q = all_q.transpose(1, 0, 2).reshape(half, width)
    both = merged + other
    left = jnp.dot(all_q, both.T, precision=HIGH) / replicas
    left = to_all(left, planes, "z").sum(0)

    right = jnp.dot(left, both, precision=HIGH) / replicas
    right = right.reshape(half, chips, share).transpose(1, 0, 2)
    right = lax.all_to_all(right, PLANE, 0, 0).sum(0)
    right = to_all(right, planes, "z").sum(0)

    halves = to_all(jnp.concatenate([right, left], 1), chips, PLANE)
    pair = lax.ppermute(halves, "core", [(0, 1), (1, 0)])
    first, second = jnp.where(core == 0, halves, pair), jnp.where(core == 0, pair, halves)
    whole = jnp.stack([first, second])
    whole = whole.transpose(0, 2, 1, 3).reshape(rank, chips, share + rows)
    left_all = whole[:, :, share:].reshape(rank, chips * rows)
    right_all = whole[:, :, :share].reshape(rank, width)
    gram = jnp.dot(left_all, left_all.T, precision=HIGH)
    lower = jnp.linalg.cholesky(gram)
    own_left = lax.dynamic_slice_in_dim(left_all, here * rows, rows, 1)
    solved = jax.scipy.linalg.solve_triangular(
        lower, jnp.concatenate([right_all, own_left], 1), lower=True
    )
    q_new, p_hat = solved[:, :width], solved[:, width:]
    approx = jnp.dot(p_hat.T, q_new, precision=HIGH)
    q_mine = lax.dynamic_slice_in_dim(q_new, here * share, share, 1).T
    return ((merged - approx)[None], q_mine)


def solution(mesh):
    split = Mesh(mesh.devices.reshape(16, 2, 4, 4), ("z", "core", "x", "y"))
    dp = ("z", "core")
    in_specs = (P(dp, PLANE, None), P(dp, PLANE, None), P(PLANE, None))
    out_specs = (P(dp, PLANE, None), P(PLANE, None))
    return jax.shard_map(
        per_device, mesh=split, in_specs=in_specs, out_specs=out_specs, check_vma=False
    )
```

```python
import functools

import jax
import jax.numpy as jnp
from jax import lax
from jax.experimental import pallas as pl
from jax.experimental.pallas import tpu as pltpu
from jax.sharding import Mesh, PartitionSpec as P

F32, BF16 = jnp.float32, jnp.bfloat16
HIGH = lax.Precision.HIGHEST
PLANE = ("z0", "shard")
SWAP = [(0, 1), (1, 0)]
VMEM = pl.BlockSpec(memory_space=pltpu.VMEM)
SMEM = pl.BlockSpec(memory_space=pltpu.SMEM)


def call(body, out, operands, specs, scratch=(), out_specs=None, flops=0):
    moved = sum(o.size * o.dtype.itemsize for o in [*operands, *out])
    return pl.pallas_call(
        body,
        out_shape=out,
        in_specs=specs,
        out_specs=out_specs or [VMEM] * len(out),
        scratch_shapes=list(scratch),
        compiler_params=pltpu.CompilerParams(vmem_limit_bytes=24 * 2**20),
        cost_estimate=pl.CostEstimate(flops=flops, bytes_accessed=moved, transcendentals=0),
    )(*operands)


def split(x, parts):
    out = []
    for _ in range(parts):
        part = x.astype(BF16)
        out.append(part)
        x = x - part.astype(F32)
    return out


def dot(a, b, dims, precision=None):
    return lax.dot_general(a, b, (dims, ((), ())), precision=precision, preferred_element_type=F32)


def left_kernel(q_ref, own_ref, other_ref, parts_ref, out_ref, q3_ref):
    shards, half, share = q_ref.shape
    rows, width = own_ref.shape
    for g in range(shards // 2):
        pair = jnp.concatenate([q_ref[2 * g], q_ref[2 * g + 1]], axis=1)
        for i, part in enumerate(split(pair, 3)):
            q3_ref[i * half : (i + 1) * half, 2 * share * g : 2 * share * (g + 1)] = part
    total = jnp.zeros((3 * half, 3 * rows), F32)
    step = width // 4
    for g in range(4):
        cols = slice(g * step, (g + 1) * step)
        for i, part in enumerate(split(own_ref[:, cols] + other_ref[:, cols], 3)):
            parts_ref[i * rows : (i + 1) * rows, cols] = part
        total = total + dot(q3_ref[:, cols], parts_ref[:, cols], ((1,), (1,)))
    block = lambda i, j: total[i * half : (i + 1) * half, j * rows : (j + 1) * rows]
    left = block(2, 0) + block(1, 1) + block(0, 2)
    left = left + (block(1, 0) + block(0, 1))
    left = left + block(0, 0)
    packed = jnp.concatenate([left[: half // 2], left[half // 2 :]], axis=1)
    out_ref[...] = jnp.broadcast_to(packed[None], out_ref.shape)


def right_kernel(replicas, z0_ref, left_ref, parts_ref, out_ref):
    packed = left_ref[0]
    for z in range(1, left_ref.shape[0]):
        packed = packed + left_ref[z]
    packed = packed * (1.0 / replicas)
    rows = packed.shape[1] // 2
    half = 2 * packed.shape[0]
    left = jnp.concatenate([packed[:, :rows], packed[:, rows:]], axis=0)
    big, mid, low = (part.astype(F32) for part in split(left, 3))
    none = jnp.zeros_like(big)
    stacked = jnp.concatenate(
        [
            jnp.concatenate([big, big, big], axis=1),
            jnp.concatenate([mid, mid, none], axis=1),
            jnp.concatenate([low, none, none], axis=1),
        ],
        axis=0,
    ).astype(BF16)
    mine = jnp.where(z0_ref[0] == 0, left[:, : rows // 2], left[:, rows // 2 :])
    width = parts_ref.shape[1]
    step = width // 8
    piece = step // 4
    for g in range(8):
        product = dot(stacked, parts_ref[:, g * step : (g + 1) * step], ((1,), (0,)))
        right = product[2 * half :] + product[half : 2 * half] + product[:half]
        right = right * (1.0 / replicas)
        for k in range(4):
            cut = right[:, k * piece : (k + 1) * piece]
            out_ref[k % 2, 2 * g + k // 2] = jnp.concatenate([cut, mine], axis=1)


def scatter_kernel(got_ref, out_ref, left_ref):
    total = jnp.zeros(got_ref.shape[2:], F32)
    for z in range(2):
        for s in range(got_ref.shape[1]):
            total = total + got_ref[z, s]
    out_ref[...] = jnp.broadcast_to(total[None], out_ref.shape)
    for g in range(got_ref.shape[1] // 2):
        four = [got_ref[k % 2, 2 * g + k // 2][:, 224:] for k in range(4)]
        left_ref[:, 128 * g : 128 * (g + 1)] = jnp.concatenate(four, axis=1)


def factor_kernel(place_ref, own_ref, other_ref, weights_ref, inverse_ref, left_ref, all_ref):
    core, here = place_ref[0], place_ref[1]
    half = own_ref.shape[0]
    rank = 2 * half
    left_ref[...] = jnp.zeros_like(left_ref)
    left_ref[pl.ds(pl.multiple_of(core * half, half), half), :] = own_ref[...]
    left_ref[pl.ds(pl.multiple_of((1 - core) * half, half), half), :] = other_ref[...]
    left = left_ref[:rank]
    work = dot(left, left_ref[...], ((1,), (1,)), HIGH)
    at_row = lax.broadcasted_iota(jnp.int32, work.shape, 0)
    at_lane = lax.broadcasted_iota(jnp.int32, work.shape, 1)
    work = jnp.where(at_lane == at_row + rank, 1.0, work)
    row_id = lax.broadcasted_iota(jnp.int32, (rank, 1), 0)
    for j in range(rank):
        row = work[j : j + 1]
        column = work[:, j : j + 1]
        scale = 1.0 / work[j : j + 1, j : j + 1]
        factor = jnp.where(row_id > j, column * scale, 0.0)
        work = work - factor * row
    pivots = jnp.sum(jnp.where(at_lane == at_row, work, 0.0), axis=1, keepdims=True)
    inverse = (work / jnp.sqrt(pivots))[:, rank : 2 * rank]
    hat = dot(left, inverse, ((0,), (1,)), HIGH)
    all_ref[...] = dot(hat, inverse, ((1,), (0,)), HIGH)
    rows = 64
    mine = all_ref[pl.ds(pl.multiple_of(here * rows, rows), rows), :]
    mine = jnp.where(core == 0, mine, jnp.concatenate([mine[:, half:], mine[:, :half]], axis=1))
    big, low = (part.astype(F32) for part in split(mine, 2))
    weights_ref[...] = jnp.concatenate(
        [
            jnp.concatenate([big, big], axis=1),
            jnp.concatenate([low, jnp.zeros_like(low)], axis=1),
        ],
        axis=0,
    ).astype(BF16)
    swapped = jnp.concatenate([inverse[:, half:], inverse[:, :half]], axis=1)
    inverse_ref[...] = jnp.where(core == 0, inverse, swapped)


def final_kernel(place_ref, own_ref, other_ref, weights_ref, inverse_ref, merged_ref, out_ref, q_ref, hold_ref, sem):
    here = place_ref[1]
    rows, width = merged_ref.shape
    piece = 224
    step = 4 * piece
    copies = []
    for g in range(width // step):
        cols = slice(g * step, (g + 1) * step)
        raw = jnp.concatenate(
            [
                jnp.concatenate([ref[k % 2, 2 * g + k // 2][:, :piece] for k in range(4)], axis=1)
                for ref in (own_ref, other_ref)
            ],
            axis=0,
        )
        product = dot(weights_ref[...], jnp.concatenate(split(raw, 2), axis=0), ((1,), (0,)))
        hold_ref[:, cols] = merged_ref[:, cols] - (product[rows:] + product[:rows])
        copy = pltpu.make_async_copy(hold_ref.at[:, cols], out_ref.at[:, cols], sem.at[g])
        copy.start()
        copies.append(copy)
    raw = jnp.concatenate(
        [
            jnp.concatenate([ref[0, here][:, :piece], ref[1, here][:, :piece]], axis=1)
            for ref in (own_ref, other_ref)
        ],
        axis=0,
    )
    q_ref[...] = dot(inverse_ref[...], raw, ((1,), (0,)), HIGH)
    for copy in copies:
        copy.wait()


def to_all(block, peers, axis):
    return lax.all_to_all(jnp.broadcast_to(block, (peers, *block.shape)), axis, 0, 0)


def per_device(grads, errors, q_prev):
    shape = jax.ShapeDtypeStruct
    rows, width = errors.shape[1:]
    share, rank = q_prev.shape
    half = rank // 2
    core, z0, here = lax.axis_index("core"), lax.axis_index("z0"), lax.axis_index("shard")
    replicas = 32

    merged = grads[0].astype(F32) + errors[0]
    own_q = lax.dynamic_slice_in_dim(q_prev.T, core * half, half, 0)
    all_q = to_all(own_q, 16, "shard")
    other = lax.ppermute(merged, "core", SWAP)

    parts, left = call(
        left_kernel,
        [shape((3 * rows, width), BF16), shape((16, 8, 128), F32)],
        [all_q, merged, other],
        [VMEM] * 3,
        [pltpu.VMEM((3 * half, width), BF16)],
        flops=2 * 48 * 192 * width,
    )
    left = lax.all_to_all(left, ("z8", "z0"), 0, 0)

    (pieces,) = call(
        functools.partial(right_kernel, replicas),
        [shape((2, 16, half, 256), F32)],
        [z0[None], left, parts],
        [SMEM, VMEM, VMEM],
        flops=2 * 48 * 192 * width,
    )
    pieces = lax.all_to_all(pieces.reshape(32, half, 256), PLANE, 0, 0).reshape(pieces.shape)
    right, left_own = call(
        scatter_kernel,
        [shape((8, half, 256), F32), shape((half, 16 * rows), F32)],
        [pieces],
        [VMEM],
    )
    right = lax.all_to_all(right, "z8", 0, 0)

    left_other = lax.ppermute(left_own, "core", SWAP)
    place = jnp.stack([core, here])
    weights, inverse = call(
        factor_kernel,
        [shape((2 * rows, 2 * rank), BF16), shape((rank, rank), F32)],
        [place, left_own, left_other],
        [SMEM, VMEM, VMEM],
        [pltpu.VMEM((128, 16 * rows), F32), pltpu.VMEM((16 * rows, rank), F32)],
        flops=10**7,
    )

    raw = to_all(right.sum(0), 32, PLANE)
    raw_other = lax.ppermute(raw, "core", SWAP)
    out, q_new = call(
        final_kernel,
        [shape((rows, width), F32), shape((rank, share), F32)],
        [place, raw.reshape(2, 16, half, 256), raw_other.reshape(2, 16, half, 256), weights, inverse, merged],
        [SMEM] + [VMEM] * 5,
        [pltpu.VMEM((rows, width), F32), pltpu.SemaphoreType.DMA((8,))],
        [pl.BlockSpec(memory_space=pl.ANY), VMEM],
        flops=2 * 128 * 64 * width,
    )
    return (out[None], q_new.T)


def solution(mesh):
    parts = Mesh(mesh.devices.reshape(8, 2, 2, 16), ("z8", "z0", "core", "shard"))
    dp = ("z8", "z0", "core")
    in_specs = (P(dp, "shard", None), P(dp, "shard", None), P("shard", None))
    out_specs = (P(dp, "shard", None), P("shard", None))
    return jax.shard_map(
        per_device, mesh=parts, in_specs=in_specs, out_specs=out_specs, check_vma=False
    )
```

```python
import functools

import jax
import jax.numpy as jnp
from jax import lax
from jax.experimental import pallas as pl
from jax.experimental.pallas import tpu as pltpu
from jax.sharding import Mesh, PartitionSpec as P

F32, BF16 = jnp.float32, jnp.bfloat16
HIGH = lax.Precision.HIGHEST
PLANE = ("z0", "shard")
SWAP = [(0, 1), (1, 0)]
VMEM = pl.BlockSpec(memory_space=pltpu.VMEM)
ANY = pl.BlockSpec(memory_space=pl.ANY)
CUTS = 8
PIECE = 224
SMEM = pl.BlockSpec(memory_space=pltpu.SMEM)


def call(body, out, operands, specs, scratch=(), out_specs=None, flops=0, limit=24):
    moved = sum(o.size * o.dtype.itemsize for o in [*operands, *out])
    return pl.pallas_call(
        body,
        out_shape=out,
        in_specs=specs,
        out_specs=out_specs or [VMEM] * len(out),
        scratch_shapes=list(scratch),
        compiler_params=pltpu.CompilerParams(vmem_limit_bytes=limit * 2**20),
        cost_estimate=pl.CostEstimate(flops=flops, bytes_accessed=moved, transcendentals=0),
    )(*operands)


def split(x, parts):
    out = []
    for _ in range(parts):
        part = x.astype(BF16)
        out.append(part)
        x = x - part.astype(F32)
    return out


def dot(a, b, dims, precision=None):
    return lax.dot_general(a, b, (dims, ((), ())), precision=precision, preferred_element_type=F32)


def ask_kernel(core_ref, q_ref, out_ref):
    half = out_ref.shape[1]
    mine = q_ref[pl.ds(pl.multiple_of(core_ref[0] * half, half), half), :]
    out_ref[...] = jnp.broadcast_to(mine[None], out_ref.shape)


def line_kernel(q_ref, out_ref):
    shards, half, share = q_ref.shape
    for g in range(shards // 2):
        pair = jnp.concatenate([q_ref[2 * g], q_ref[2 * g + 1]], axis=1)
        for i, part in enumerate(split(pair, 3)):
            out_ref[i * half : (i + 1) * half, 2 * share * g : 2 * share * (g + 1)] = part


def left_kernel(q_ref, own_ref, other_ref, parts_ref, out_ref, own_buf, other_buf, parts_buf, in_sem, out_sem):
    half = q_ref.shape[0] // 3
    rows, width = own_ref.shape
    step = width // CUTS
    cuts = [slice(g * step, (g + 1) * step) for g in range(CUTS)]
    loads, stores = [], []
    for g, cols in enumerate(cuts):
        pair = [(own_ref, own_buf), (other_ref, other_buf)]
        loads.append(
            [pltpu.make_async_copy(r.at[:, cols], b.at[:, cols], in_sem.at[i, g]) for i, (r, b) in enumerate(pair)]
        )
        for load in loads[-1]:
            load.start()
    total = jnp.zeros((3 * half, 3 * rows), F32)
    for g, cols in enumerate(cuts):
        for load in loads[g]:
            load.wait()
        for i, part in enumerate(split(own_buf[:, cols] + other_buf[:, cols], 3)):
            parts_buf[i * rows : (i + 1) * rows, cols] = part
        stores.append(pltpu.make_async_copy(parts_buf.at[:, cols], parts_ref.at[:, cols], out_sem.at[g]))
        stores[-1].start()
        total = total + dot(q_ref[:, cols], parts_buf[:, cols], ((1,), (1,)))
    block = lambda i, j: total[i * half : (i + 1) * half, j * rows : (j + 1) * rows]
    left = block(2, 0) + block(1, 1) + block(0, 2)
    left = left + (block(1, 0) + block(0, 1))
    left = left + block(0, 0)
    packed = jnp.concatenate([left[: half // 2], left[half // 2 :]], axis=1)
    out_ref[...] = jnp.broadcast_to(packed[None], out_ref.shape)
    for store in stores:
        store.wait()


def right_kernel(replicas, z0_ref, left_ref, parts_ref, out_ref, parts_buf, sem):
    width = parts_ref.shape[1]
    step = width // 8
    piece = step // 4
    loads = []
    for g in range(8):
        cols = slice(g * step, (g + 1) * step)
        loads.append(pltpu.make_async_copy(parts_ref.at[:, cols], parts_buf.at[:, cols], sem.at[g]))
        loads[-1].start()
    packed = left_ref[0]
    for z in range(1, left_ref.shape[0]):
        packed = packed + left_ref[z]
    packed = packed * (1.0 / replicas)
    rows = packed.shape[1] // 2
    half = 2 * packed.shape[0]
    left = jnp.concatenate([packed[:, :rows], packed[:, rows:]], axis=0)
    big, mid, low = (part.astype(F32) for part in split(left, 3))
    none = jnp.zeros_like(big)
    stacked = jnp.concatenate(
        [
            jnp.concatenate([big, big, big], axis=1),
            jnp.concatenate([mid, mid, none], axis=1),
            jnp.concatenate([low, none, none], axis=1),
        ],
        axis=0,
    ).astype(BF16)
    mine = jnp.where(z0_ref[0] == 0, left[:, : rows // 2], left[:, rows // 2 :])
    for g in range(8):
        loads[g].wait()
        product = dot(stacked, parts_buf[:, g * step : (g + 1) * step], ((1,), (0,)))
        right = product[2 * half :] + product[half : 2 * half] + product[:half]
        right = right * (1.0 / replicas)
        for k in range(4):
            cut = right[:, k * piece : (k + 1) * piece]
            out_ref[k % 2, 2 * g + k // 2] = jnp.concatenate([cut, mine], axis=1)


def scatter_kernel(got_ref, out_ref, left_ref):
    total = jnp.zeros(got_ref.shape[2:], F32)
    for z in range(2):
        for s in range(got_ref.shape[1]):
            total = total + got_ref[z, s]
    out_ref[...] = jnp.broadcast_to(total[None, :, :PIECE], out_ref.shape)
    for g in range(got_ref.shape[1] // 2):
        four = [got_ref[k % 2, 2 * g + k // 2][:, PIECE:] for k in range(4)]
        left_ref[:, 128 * g : 128 * (g + 1)] = jnp.concatenate(four, axis=1)


def spread_kernel(got_ref, weights_ref, inverse_ref, out_ref):
    total = got_ref[0]
    for z in range(1, got_ref.shape[0]):
        total = total + got_ref[z]
    out_ref[...] = jnp.broadcast_to(total[None], out_ref.shape)


def factor_kernel(place_ref, own_ref, other_ref, weights_ref, inverse_ref, left_ref, all_ref):
    core, here = place_ref[0], place_ref[1]
    half = own_ref.shape[0]
    rank = 2 * half
    left_ref[...] = jnp.zeros_like(left_ref)
    left_ref[pl.ds(pl.multiple_of(core * half, half), half), :] = own_ref[...]
    left_ref[pl.ds(pl.multiple_of((1 - core) * half, half), half), :] = other_ref[...]
    left = left_ref[:rank]
    work = dot(left, left_ref[...], ((1,), (1,)), HIGH)
    at_row = lax.broadcasted_iota(jnp.int32, work.shape, 0)
    at_lane = lax.broadcasted_iota(jnp.int32, work.shape, 1)
    work = jnp.where(at_lane == at_row + rank, 1.0, work)
    row_id = lax.broadcasted_iota(jnp.int32, (rank, 1), 0)
    for j in range(rank):
        row = work[j : j + 1]
        column = work[:, j : j + 1]
        scale = 1.0 / work[j : j + 1, j : j + 1]
        factor = jnp.where(row_id > j, column * scale, 0.0)
        work = work - factor * row
    pivots = jnp.sum(jnp.where(at_lane == at_row, work, 0.0), axis=1, keepdims=True)
    inverse = (work / jnp.sqrt(pivots))[:, rank : 2 * rank]
    hat = dot(left, inverse, ((0,), (1,)), HIGH)
    all_ref[...] = dot(hat, inverse, ((1,), (0,)), HIGH)
    rows = 64
    mine = all_ref[pl.ds(pl.multiple_of(here * rows, rows), rows), :]
    big, low = (part.astype(F32) for part in split(mine, 2))
    weights_ref[...] = jnp.concatenate(
        [
            jnp.concatenate([big, big], axis=1),
            jnp.concatenate([low, jnp.zeros_like(low)], axis=1),
        ],
        axis=0,
    ).astype(BF16)
    inverse_ref[...] = inverse


def final_kernel(place_ref, raw_ref, weights_ref, inverse_ref, grads_ref, errors_ref, out_ref, q_ref, hold_ref, sem):
    here = place_ref[1]
    rows, width = hold_ref.shape
    step = 4 * PIECE
    copies = []
    for g in range(width // step):
        cols = slice(g * step, (g + 1) * step)
        raw = jnp.concatenate(
            [
                jnp.concatenate([raw_ref[core, k % 2, 2 * g + k // 2] for k in range(4)], axis=1)
                for core in range(2)
            ],
            axis=0,
        )
        product = dot(weights_ref[...], jnp.concatenate(split(raw, 2), axis=0), ((1,), (0,)))
        merged = grads_ref[0, :, cols].astype(F32) + errors_ref[0, :, cols]
        hold_ref[:, cols] = merged - (product[rows:] + product[:rows])
        copy = pltpu.make_async_copy(hold_ref.at[:, cols], out_ref.at[:, cols], sem.at[g])
        copy.start()
        copies.append(copy)
    raw = jnp.concatenate(
        [
            jnp.concatenate([raw_ref[core, 0, here], raw_ref[core, 1, here]], axis=1)
            for core in range(2)
        ],
        axis=0,
    )
    q_ref[...] = dot(inverse_ref[...], raw, ((1,), (0,)), HIGH)
    for copy in copies:
        copy.wait()


def to_all(block, peers, axis):
    return lax.all_to_all(jnp.broadcast_to(block, (peers, *block.shape)), axis, 0, 0)


def per_device(grads, errors, q_prev):
    shape = jax.ShapeDtypeStruct
    rows, width = errors.shape[1:]
    share, rank = q_prev.shape
    half = rank // 2
    core, z0, here = lax.axis_index("core"), lax.axis_index("z0"), lax.axis_index("shard")
    replicas = 32

    (own_q,) = call(
        ask_kernel,
        [shape((16, half, share), F32)],
        [core[None], q_prev.T],
        [SMEM, VMEM],
    )
    all_q = lax.all_to_all(own_q, "shard", 0, 0)
    merged = grads[0].astype(F32) + errors[0]
    other = lax.ppermute(merged, "core", SWAP)
    (all_q,) = call(
        line_kernel,
        [shape((3 * half, width), BF16)],
        [all_q],
        [VMEM],
        flops=10**11,
    )
    parts, left = call(
        left_kernel,
        [shape((3 * rows, width), BF16), shape((16, 8, 128), F32)],
        [all_q, merged, other],
        [VMEM, ANY, ANY],
        [
            pltpu.VMEM((rows, width), F32),
            pltpu.VMEM((rows, width), F32),
            pltpu.VMEM((3 * rows, width), BF16),
            pltpu.SemaphoreType.DMA((2, CUTS)),
            pltpu.SemaphoreType.DMA((CUTS,)),
        ],
        [ANY, VMEM],
        flops=2 * 48 * 192 * width,
        limit=52,
    )
    left = lax.all_to_all(left, ("z8", "z0"), 0, 0)

    (pieces,) = call(
        functools.partial(right_kernel, replicas),
        [shape((2, 16, half, 256), F32)],
        [z0[None], left, parts],
        [SMEM, VMEM, ANY],
        [pltpu.VMEM((3 * rows, width), BF16), pltpu.SemaphoreType.DMA((8,))],
        flops=2 * 48 * 192 * width,
        limit=52,
    )
    pieces = lax.all_to_all(pieces.reshape(32, half, 256), PLANE, 0, 0).reshape(pieces.shape)
    right, left_own = call(
        scatter_kernel,
        [shape((8, half, PIECE), F32), shape((half, 16 * rows), F32)],
        [pieces],
        [VMEM],
    )
    right = lax.all_to_all(right, "z8", 0, 0)

    left_other = lax.ppermute(left_own, "core", SWAP)
    place = jnp.stack([core, here])
    weights, inverse = call(
        factor_kernel,
        [shape((2 * rows, 2 * rank), BF16), shape((rank, rank), F32)],
        [place, left_own, left_other],
        [SMEM, VMEM, VMEM],
        [pltpu.VMEM((128, 16 * rows), F32), pltpu.VMEM((16 * rows, rank), F32)],
        flops=10**7,
    )

    (raw,) = call(
        spread_kernel, [shape((32, half, PIECE), F32)], [right, weights, inverse], [VMEM] * 3
    )
    raw = lax.all_to_all(raw, PLANE, 0, 0)
    raw = lax.all_gather(raw, "core").reshape(2, 2, 16, half, PIECE)
    out, q_new = call(
        final_kernel,
        [shape((rows, width), F32), shape((rank, share), F32)],
        [place, raw, weights, inverse, grads, errors],
        [SMEM] + [VMEM] * 5,
        [pltpu.VMEM((rows, width), F32), pltpu.SemaphoreType.DMA((8,))],
        [pl.BlockSpec(memory_space=pl.ANY), VMEM],
        flops=2 * 128 * 64 * width,
    )
    return (out[None], q_new.T)


def solution(mesh):
    parts = Mesh(mesh.devices.reshape(8, 2, 2, 16), ("z8", "z0", "core", "shard"))
    dp = ("z8", "z0", "core")
    in_specs = (P(dp, "shard", None), P(dp, "shard", None), P("shard", None))
    out_specs = (P(dp, "shard", None), P("shard", None))
    return jax.shard_map(
        per_device, mesh=parts, in_specs=in_specs, out_specs=out_specs, check_vma=False
    )
```

```python
import functools

import jax
import jax.numpy as jnp
from jax import lax
from jax.experimental import pallas as pl
from jax.experimental.pallas import tpu as pltpu
from jax.sharding import Mesh, PartitionSpec as P

F32, BF16 = jnp.float32, jnp.bfloat16
HIGH = lax.Precision.HIGHEST
PLANE = ("z0", "shard")
SWAP = [(0, 1), (1, 0)]
VMEM = pl.BlockSpec(memory_space=pltpu.VMEM)
ANY = pl.BlockSpec(memory_space=pl.ANY)
CUTS = 8
STRIDE = 4
PIECE = 224
SMEM = pl.BlockSpec(memory_space=pltpu.SMEM)


def call(body, out, operands, specs, scratch=(), out_specs=None, flops=0, limit=24):
    moved = sum(o.size * o.dtype.itemsize for o in [*operands, *out])
    return pl.pallas_call(
        body,
        out_shape=out,
        in_specs=specs,
        out_specs=out_specs or [VMEM] * len(out),
        scratch_shapes=list(scratch),
        compiler_params=pltpu.CompilerParams(vmem_limit_bytes=limit * 2**20),
        cost_estimate=pl.CostEstimate(flops=flops, bytes_accessed=moved, transcendentals=0),
    )(*operands)


def split(x, parts):
    out = []
    for _ in range(parts):
        part = x.astype(BF16)
        out.append(part)
        x = x - part.astype(F32)
    return out


def dot(a, b, dims, precision=None):
    return lax.dot_general(a, b, (dims, ((), ())), precision=precision, preferred_element_type=F32)


def ask_kernel(place_ref, q_ref, out_ref):
    half = out_ref.shape[1]
    mine = q_ref[pl.ds(pl.multiple_of(place_ref[0] * half, half), half), :]
    out_ref[...] = jnp.broadcast_to(mine[None], out_ref.shape)


def line_kernel(q_ref, out_ref):
    shards, half, share = q_ref.shape
    for g in range(shards // 2):
        pair = jnp.concatenate([q_ref[2 * g], q_ref[2 * g + 1]], axis=1)
        for i, part in enumerate(split(pair, 2)):
            out_ref[i * half : (i + 1) * half, 2 * share * g : 2 * share * (g + 1)] = part


def left_kernel(q_ref, own_ref, other_ref, parts_ref, out_ref, other_buf, sem):
    half = q_ref.shape[0] // 2
    rows, width = own_ref.shape
    step = width // CUTS
    cuts = [slice(g * step, (g + 1) * step) for g in range(CUTS)]
    loads = []
    for g, cols in enumerate(cuts):
        loads.append(pltpu.make_async_copy(other_ref.at[:, cols], other_buf.at[:, cols], sem.at[g]))
        loads[-1].start()
    total = jnp.zeros((2 * half, 2 * rows), F32)
    for g, cols in enumerate(cuts):
        loads[g].wait()
        for i, part in enumerate(split(own_ref[:, cols] + other_buf[:, cols], 2)):
            parts_ref[i * rows : (i + 1) * rows, cols] = part
        total = total + dot(q_ref[:, cols], parts_ref[:, cols], ((1,), (1,)))
    left = total[half:, rows:] + total[half:, :rows] + total[:half, rows:]
    left = left + total[:half, :rows]
    packed = jnp.concatenate([left[: half // 2], left[half // 2 :]], axis=1)
    out_ref[...] = jnp.broadcast_to(packed[None], out_ref.shape)


def right_kernel(replicas, place_ref, left_ref, parts_ref, out_ref, mine_ref):
    width = parts_ref.shape[1]
    step = width // 8
    piece = step // 4
    packed = left_ref[0]
    for z in range(1, left_ref.shape[0]):
        packed = packed + left_ref[z]
    packed = packed * (1.0 / replicas)
    rows = packed.shape[1] // 2
    half = 2 * packed.shape[0]
    left = jnp.concatenate([packed[:, :rows], packed[:, rows:]], axis=0)
    mine_ref[...] = left
    big, low = (part.astype(F32) for part in split(left, 2))
    stacked = jnp.concatenate(
        [jnp.concatenate([big, big], axis=1), jnp.concatenate([low, low], axis=1)], axis=0
    ).astype(BF16)
    mine = jnp.where(place_ref[2] == 0, left[:, : rows // 2], left[:, rows // 2 :])
    for g in range(8):
        product = dot(stacked, parts_ref[:, g * step : (g + 1) * step], ((1,), (0,)))
        right = (product[half:] + product[:half]) * (1.0 / replicas)
        for k in range(4):
            cut = right[:, k * piece : (k + 1) * piece]
            out_ref[k % 2, 2 * g + k // 2] = jnp.concatenate([cut, mine], axis=1)


def scatter_kernel(got_ref, out_ref, left_ref):
    total = jnp.zeros(got_ref.shape[2:], F32)
    for z in range(2):
        for s in range(got_ref.shape[1]):
            total = total + got_ref[z, s]
    out_ref[...] = jnp.broadcast_to(total[None, :, :PIECE], out_ref.shape)
    for g in range(got_ref.shape[1] // 2):
        four = [got_ref[k % 2, 2 * g + k // 2][:, PIECE:] for k in range(4)]
        left_ref[:, 128 * g : 128 * (g + 1)] = jnp.concatenate(four, axis=1)


def spread_kernel(got_ref, weights_ref, inverse_ref, out_ref):
    total = got_ref[0]
    for z in range(1, got_ref.shape[0]):
        total = total + got_ref[z]
    out_ref[...] = jnp.broadcast_to(total[None], out_ref.shape)


def factor_kernel(place_ref, own_ref, other_ref, mine_ref, weights_ref, inverse_ref, left_ref, both_ref):
    core, here = place_ref[0], place_ref[1]
    half, rows = mine_ref.shape
    rank = 2 * half
    first = pl.ds(pl.multiple_of(core * half, half), half)
    second = pl.ds(pl.multiple_of((1 - core) * half, half), half)
    left_ref[first, :] = own_ref[...]
    left_ref[second, :] = other_ref[...]
    pair = other_ref[:, pl.ds(pl.multiple_of(here // 2 * 2 * rows, 2 * rows), 2 * rows)]
    both_ref[first, :] = mine_ref[...]
    both_ref[second, :] = jnp.where(here % 2 == 0, pair[:, :rows], pair[:, rows:])
    parts = jnp.concatenate(split(left_ref[...], 3), axis=0)
    products = dot(parts, parts, ((1,), (1,)))
    block = lambda i, j: products[i * rank : (i + 1) * rank, j * rank : (j + 1) * rank]
    gram = block(2, 0) + block(1, 1) + block(0, 2)
    gram = gram + (block(1, 0) + block(0, 1))
    gram = gram + block(0, 0)
    at_row = lax.broadcasted_iota(jnp.int32, (rank, 4 * rank), 0)
    at_lane = lax.broadcasted_iota(jnp.int32, (rank, 4 * rank), 1)
    work = jnp.concatenate([gram, jnp.zeros((rank, rank), F32), both_ref[...]], axis=1)
    work = jnp.where(at_lane == at_row + rank, 1.0, work)
    for start in range(0, rank, STRIDE):
        columns = [jnp.broadcast_to(work[:, j : j + 1], work.shape) for j in range(start, start + STRIDE)]
        for t in range(STRIDE):
            j = start + t
            factor = jnp.where(at_row > j, columns[t] * (1.0 / columns[t][j : j + 1]), 0.0)
            for u in range(t + 1, STRIDE):
                columns[u] = columns[u] - factor * columns[u][j : j + 1]
            work = work - factor * work[j : j + 1]
    pivots = jnp.sum(jnp.where(at_lane == at_row, work, 0.0), axis=1, keepdims=True)
    work = work / jnp.sqrt(pivots)
    inverse = work[:, rank : 2 * rank]
    mine = dot(work[:, 2 * rank :], inverse, ((0,), (0,)), HIGH)
    big, low = (part.astype(F32) for part in split(mine, 2))
    weights_ref[...] = jnp.concatenate(
        [jnp.concatenate([big, big], axis=1), jnp.concatenate([low, low], axis=1)], axis=0
    ).astype(BF16)
    inverse_ref[...] = inverse


def final_kernel(place_ref, raw_ref, weights_ref, inverse_ref, grads_ref, errors_ref, out_ref, q_ref, hold_ref, sem):
    here = place_ref[1]
    rows, width = hold_ref.shape
    step = 4 * PIECE
    copies = []
    for g in range(width // step):
        cols = slice(g * step, (g + 1) * step)
        raw = jnp.concatenate(
            [
                jnp.concatenate([raw_ref[core, k % 2, 2 * g + k // 2] for k in range(4)], axis=1)
                for core in range(2)
            ],
            axis=0,
        )
        product = dot(weights_ref[...], jnp.concatenate(split(raw, 2), axis=0), ((1,), (0,)))
        merged = grads_ref[0, :, cols].astype(F32) + errors_ref[0, :, cols]
        hold_ref[:, cols] = merged - (product[rows:] + product[:rows])
        copy = pltpu.make_async_copy(hold_ref.at[:, cols], out_ref.at[:, cols], sem.at[g])
        copy.start()
        copies.append(copy)
    raw = jnp.concatenate(
        [
            jnp.concatenate([raw_ref[core, 0, here], raw_ref[core, 1, here]], axis=1)
            for core in range(2)
        ],
        axis=0,
    )
    q_ref[...] = dot(inverse_ref[...], raw, ((1,), (0,)), HIGH)
    for copy in copies:
        copy.wait()


def to_all(block, peers, axis):
    return lax.all_to_all(jnp.broadcast_to(block, (peers, *block.shape)), axis, 0, 0)


def per_device(grads, errors, q_prev):
    shape = jax.ShapeDtypeStruct
    rows, width = errors.shape[1:]
    share, rank = q_prev.shape
    half = rank // 2
    place = jnp.stack([lax.axis_index(axis) for axis in ("core", "shard", "z0")])
    replicas = 32

    (own_q,) = call(
        ask_kernel,
        [shape((16, half, share), F32)],
        [place, q_prev.T],
        [SMEM, VMEM],
    )
    all_q = lax.all_to_all(own_q, "shard", 0, 0)
    merged = grads[0].astype(F32) + errors[0]
    other = lax.ppermute(merged, "core", SWAP)
    (all_q,) = call(
        line_kernel,
        [shape((2 * half, width), BF16)],
        [all_q],
        [VMEM],
        flops=10**11,
    )
    parts, left = call(
        left_kernel,
        [shape((2 * rows, width), BF16), shape((16, 8, 128), F32)],
        [all_q, merged, other],
        [VMEM, VMEM, ANY],
        [pltpu.VMEM((rows, width), F32), pltpu.SemaphoreType.DMA((CUTS,))],
        flops=2 * 32 * 128 * width,
    )
    left = lax.all_to_all(left, ("z8", "z0"), 0, 0)

    pieces, mine = call(
        functools.partial(right_kernel, replicas),
        [shape((2, 16, half, 256), F32), shape((half, rows), F32)],
        [place, left, parts],
        [SMEM, VMEM, VMEM],
        flops=2 * 32 * 128 * width,
    )
    pieces = lax.all_to_all(pieces.reshape(32, half, 256), PLANE, 0, 0).reshape(pieces.shape)
    right, left_own = call(
        scatter_kernel,
        [shape((8, half, PIECE), F32), shape((half, 16 * rows), F32)],
        [pieces],
        [VMEM],
    )
    right = lax.all_to_all(right, "z8", 0, 0)

    left_other = lax.ppermute(left_own, "core", SWAP)
    weights, inverse = call(
        factor_kernel,
        [shape((2 * rows, 2 * rank), BF16), shape((rank, rank), F32)],
        [place, left_own, left_other, mine],
        [SMEM] + [VMEM] * 3,
        [pltpu.VMEM((rank, 16 * rows), F32), pltpu.VMEM((rank, rows), F32)],
        flops=10**7,
    )

    (raw,) = call(
        spread_kernel, [shape((32, half, PIECE), F32)], [right, weights, inverse], [VMEM] * 3
    )
    raw = lax.all_to_all(raw, PLANE, 0, 0)
    raw = lax.all_gather(raw, "core").reshape(2, 2, 16, half, PIECE)
    out, q_new = call(
        final_kernel,
        [shape((rows, width), F32), shape((rank, share), F32)],
        [place, raw, weights, inverse, grads, errors],
        [SMEM] + [VMEM] * 5,
        [pltpu.VMEM((rows, width), F32), pltpu.SemaphoreType.DMA((8,))],
        [pl.BlockSpec(memory_space=pl.ANY), VMEM],
        flops=2 * 128 * 64 * width,
    )
    return (out[None], q_new.T)


def solution(mesh):
    parts = Mesh(mesh.devices.reshape(8, 2, 2, 16), ("z8", "z0", "core", "shard"))
    dp = ("z8", "z0", "core")
    in_specs = (P(dp, "shard", None), P(dp, "shard", None), P("shard", None))
    out_specs = (P(dp, "shard", None), P("shard", None))
    return jax.shard_map(
        per_device, mesh=parts, in_specs=in_specs, out_specs=out_specs, check_vma=False
    )
```

```python
import functools

import jax
import jax.numpy as jnp
from jax import lax
from jax.experimental import pallas as pl
from jax.experimental.pallas import tpu as pltpu
from jax.sharding import Mesh, PartitionSpec as P

F32, BF16 = jnp.float32, jnp.bfloat16
HIGH = lax.Precision.HIGHEST
PLANE = ("z0", "shard")
SWAP = [(0, 1), (1, 0)]
VMEM = pl.BlockSpec(memory_space=pltpu.VMEM)
ANY = pl.BlockSpec(memory_space=pl.ANY)
CUTS = 7
STRIDE = 4
SMEM = pl.BlockSpec(memory_space=pltpu.SMEM)


def call(body, out, operands, specs, scratch=(), out_specs=None, flops=0, limit=24):
    moved = sum(o.size * o.dtype.itemsize for o in [*operands, *out])
    return pl.pallas_call(
        body,
        out_shape=out,
        in_specs=specs,
        out_specs=out_specs or [VMEM] * len(out),
        scratch_shapes=list(scratch),
        compiler_params=pltpu.CompilerParams(vmem_limit_bytes=limit * 2**20),
        cost_estimate=pl.CostEstimate(flops=flops, bytes_accessed=moved, transcendentals=0),
    )(*operands)


def split(x, parts):
    out = []
    for _ in range(parts):
        part = x.astype(BF16)
        out.append(part)
        x = x - part.astype(F32)
    return out


def dot(a, b, dims, precision=None):
    return lax.dot_general(a, b, (dims, ((), ())), precision=precision, preferred_element_type=F32)


def ask_kernel(place_ref, q_ref, out_ref):
    half = q_ref.shape[0] // 2
    mine = q_ref[pl.ds(pl.multiple_of(place_ref[0] * half, half), half), :]
    packed = jnp.concatenate([mine[: half // 2], mine[half // 2 :]], axis=1)
    out_ref[...] = jnp.broadcast_to(packed[None], out_ref.shape)


def line_kernel(q_ref, out_ref):
    shards, low, span = q_ref.shape
    share = span // 2
    for g in range(shards // 2):
        a, b = q_ref[2 * g], q_ref[2 * g + 1]
        pair = jnp.concatenate(
            [
                jnp.concatenate([a[:, :share], b[:, :share]], axis=1),
                jnp.concatenate([a[:, share:], b[:, share:]], axis=1),
            ],
            axis=0,
        )
        for i, part in enumerate(split(pair, 2)):
            out_ref[2 * low * i : 2 * low * (i + 1), span * g : span * (g + 1)] = part


def left_kernel(q_ref, own_ref, other_ref, parts_ref, out_ref, other_buf, sem):
    half = q_ref.shape[0] // 2
    rows, width = own_ref.shape
    step = width // CUTS
    cuts = [slice(g * step, (g + 1) * step) for g in range(CUTS)]
    loads = []
    for g, cols in enumerate(cuts):
        loads.append(pltpu.make_async_copy(other_ref.at[:, cols], other_buf.at[:, cols], sem.at[g]))
        loads[-1].start()
    total = jnp.zeros((2 * half, 2 * rows), F32)
    for g, cols in enumerate(cuts):
        loads[g].wait()
        for i, part in enumerate(split(own_ref[:, cols] + other_buf[:, cols], 2)):
            parts_ref[i * rows : (i + 1) * rows, cols] = part
        total = total + dot(q_ref[:, cols], parts_ref[:, cols], ((1,), (1,)))
    left = total[half:, rows:] + total[half:, :rows] + total[:half, rows:]
    left = left + total[:half, :rows]
    packed = jnp.concatenate([left[: half // 2], left[half // 2 :]], axis=1)
    out_ref[...] = jnp.broadcast_to(packed[None], out_ref.shape)


def right_kernel(replicas, place_ref, left_ref, parts_ref, out_ref, mine_ref):
    width = parts_ref.shape[1]
    step = width // 8
    share = step // 2
    packed = left_ref[0]
    for z in range(1, left_ref.shape[0]):
        packed = packed + left_ref[z]
    packed = packed * (1.0 / replicas)
    rows = packed.shape[1] // 2
    half = 2 * packed.shape[0]
    left = jnp.concatenate([packed[:, :rows], packed[:, rows:]], axis=0)
    mine_ref[...] = left
    big, low = (part.astype(F32) for part in split(left, 2))
    stacked = jnp.concatenate(
        [jnp.concatenate([big, big], axis=1), jnp.concatenate([low, low], axis=1)], axis=0
    ).astype(BF16)
    mine = jnp.where(place_ref[2] == 0, left[: half // 2], left[half // 2 :])
    mine = jnp.concatenate([mine, mine], axis=0)
    for g in range(8):
        product = dot(stacked, parts_ref[:, g * step : (g + 1) * step], ((1,), (0,)))
        right = (product[half:] + product[:half]) * (1.0 / replicas)
        for k in range(2):
            cut = jnp.concatenate([right[:, k * share : (k + 1) * share], mine], axis=1)
            out_ref[0, 2 * g + k] = cut[: half // 2]
            out_ref[1, 2 * g + k] = cut[half // 2 :]


def scatter_kernel(got_ref, out_ref, left_ref):
    total = got_ref[0, 0]
    for s in range(1, got_ref.shape[1]):
        total = total + got_ref[0, s]
    for s in range(got_ref.shape[1]):
        total = total + got_ref[1, s]
    share = out_ref.shape[2]
    out_ref[...] = jnp.broadcast_to(total[None, :, :share], out_ref.shape)
    low, rows = got_ref.shape[2], got_ref.shape[3] - share
    for z in range(2):
        for g in range(got_ref.shape[1] // 2):
            pair = [got_ref[z, 2 * g + k][:, share:] for k in range(2)]
            left_ref[low * z : low * (z + 1), 2 * rows * g : 2 * rows * (g + 1)] = jnp.concatenate(pair, axis=1)


def spread_kernel(got_ref, weights_ref, inverse_ref, out_ref):
    total = got_ref[0]
    for z in range(1, got_ref.shape[0]):
        total = total + got_ref[z]
    out_ref[...] = jnp.broadcast_to(total[None], out_ref.shape)


def factor_kernel(place_ref, own_ref, other_ref, mine_ref, weights_ref, inverse_ref, left_ref, both_ref):
    core, here = place_ref[0], place_ref[1]
    half, rows = mine_ref.shape
    rank = 2 * half
    first = pl.ds(pl.multiple_of(core * half, half), half)
    second = pl.ds(pl.multiple_of((1 - core) * half, half), half)
    left_ref[first, :] = own_ref[...]
    left_ref[second, :] = other_ref[...]
    pair = other_ref[:, pl.ds(pl.multiple_of(here // 2 * 2 * rows, 2 * rows), 2 * rows)]
    both_ref[first, :] = mine_ref[...]
    both_ref[second, :] = jnp.where(here % 2 == 0, pair[:, :rows], pair[:, rows:])
    parts = jnp.concatenate(split(left_ref[...], 3), axis=0)
    products = dot(parts, parts, ((1,), (1,)))
    block = lambda i, j: products[i * rank : (i + 1) * rank, j * rank : (j + 1) * rank]
    gram = block(2, 0) + block(1, 1) + block(0, 2)
    gram = gram + (block(1, 0) + block(0, 1))
    gram = gram + block(0, 0)
    at_row = lax.broadcasted_iota(jnp.int32, (rank, 4 * rank), 0)
    at_lane = lax.broadcasted_iota(jnp.int32, (rank, 4 * rank), 1)
    work = jnp.concatenate([gram, jnp.zeros((rank, rank), F32), both_ref[...]], axis=1)
    work = jnp.where(at_lane == at_row + rank, 1.0, work)
    for start in range(0, rank, STRIDE):
        columns = [jnp.broadcast_to(work[:, j : j + 1], work.shape) for j in range(start, start + STRIDE)]
        for t in range(STRIDE):
            j = start + t
            factor = jnp.where(at_row > j, columns[t] * (1.0 / columns[t][j : j + 1]), 0.0)
            for u in range(t + 1, STRIDE):
                columns[u] = columns[u] - factor * columns[u][j : j + 1]
            work = work - factor * work[j : j + 1]
    pivots = jnp.sum(jnp.where(at_lane == at_row, work, 0.0), axis=1, keepdims=True)
    work = work / jnp.sqrt(pivots)
    inverse = work[:, rank : 2 * rank]
    mine = dot(work[:, 2 * rank :], inverse, ((0,), (0,)), HIGH)
    big, low = (part.astype(F32) for part in split(mine, 2))
    weights_ref[...] = jnp.concatenate(
        [jnp.concatenate([big, big], axis=1), jnp.concatenate([low, low], axis=1)], axis=0
    ).astype(BF16)
    inverse_ref[...] = inverse


def final_kernel(place_ref, raw_ref, weights_ref, inverse_ref, merged_ref, out_ref, q_ref, hold_ref, sem):
    here = place_ref[1]
    rows, width = hold_ref.shape
    share = raw_ref.shape[-1]
    step = 2 * share
    copies = []
    for g in range(width // step):
        cols = slice(g * step, (g + 1) * step)
        raw = jnp.concatenate(
            [
                jnp.concatenate([raw_ref[core, z, 2 * g], raw_ref[core, z, 2 * g + 1]], axis=1)
                for core in range(2)
                for z in range(2)
            ],
            axis=0,
        )
        product = dot(weights_ref[...], jnp.concatenate(split(raw, 2), axis=0), ((1,), (0,)))
        hold_ref[:, cols] = merged_ref[:, cols] - (product[rows:] + product[:rows])
        copy = pltpu.make_async_copy(hold_ref.at[:, cols], out_ref.at[:, cols], sem.at[g])
        copy.start()
        copies.append(copy)
    raw = jnp.concatenate([raw_ref[core, z, here] for core in range(2) for z in range(2)], axis=0)
    q_ref[...] = dot(inverse_ref[...], raw, ((1,), (0,)), HIGH)
    for copy in copies:
        copy.wait()


def per_device(grads, errors, q_prev):
    shape = jax.ShapeDtypeStruct
    rows, width = errors.shape[1:]
    share, rank = q_prev.shape
    half = rank // 2
    place = jnp.stack([lax.axis_index(axis) for axis in ("core", "shard", "z0")])
    replicas = 32

    (own_q,) = call(
        ask_kernel,
        [shape((16, half // 2, 2 * share), F32)],
        [place, q_prev.T],
        [SMEM, VMEM],
    )
    all_q = lax.all_to_all(own_q, "shard", 0, 0)
    merged = grads[0].astype(F32) + errors[0]
    other = lax.ppermute(merged, "core", SWAP)
    (all_q,) = call(
        line_kernel,
        [shape((2 * half, width), BF16)],
        [all_q],
        [VMEM],
        flops=10**11,
    )
    parts, left = call(
        left_kernel,
        [shape((2 * rows, width), BF16), shape((16, 8, 128), F32)],
        [all_q, merged, other],
        [VMEM, VMEM, ANY],
        [pltpu.VMEM((rows, width), F32), pltpu.SemaphoreType.DMA((CUTS,))],
        flops=2 * 32 * 128 * width,
    )
    left = lax.all_to_all(left, ("z8", "z0"), 0, 0)

    pieces, mine = call(
        functools.partial(right_kernel, replicas),
        [shape((2, 16, half // 2, 512), F32), shape((half, rows), F32)],
        [place, left, parts],
        [SMEM, VMEM, VMEM],
        flops=2 * 32 * 128 * width,
    )
    pieces = lax.all_to_all(pieces.reshape(32, half // 2, 512), PLANE, 0, 0).reshape(pieces.shape)
    right, left_own = call(
        scatter_kernel,
        [shape((8, half // 2, share), F32), shape((half, 16 * rows), F32)],
        [pieces],
        [VMEM],
    )
    right = lax.all_to_all(right, "z8", 0, 0)

    left_other = lax.ppermute(left_own, "core", SWAP)
    weights, inverse = call(
        factor_kernel,
        [shape((2 * rows, 2 * rank), BF16), shape((rank, rank), F32)],
        [place, left_own, left_other, mine],
        [SMEM] + [VMEM] * 3,
        [pltpu.VMEM((rank, 16 * rows), F32), pltpu.VMEM((rank, rows), F32)],
        flops=10**7,
    )

    (raw,) = call(
        spread_kernel, [shape((32, half // 2, share), F32)], [right, weights, inverse], [VMEM] * 3
    )
    raw = lax.all_to_all(raw, PLANE, 0, 0)
    raw = lax.all_gather(raw, "core").reshape(2, 2, 16, half // 2, share)
    out, q_new = call(
        final_kernel,
        [shape((rows, width), F32), shape((rank, share), F32)],
        [place, raw, weights, inverse, merged],
        [SMEM] + [VMEM] * 4,
        [pltpu.VMEM((rows, width), F32), pltpu.SemaphoreType.DMA((8,))],
        [pl.BlockSpec(memory_space=pl.ANY), VMEM],
        flops=2 * 128 * 64 * width,
    )
    return (out[None], q_new.T)


def solution(mesh):
    parts = Mesh(mesh.devices.reshape(8, 2, 2, 16), ("z8", "z0", "core", "shard"))
    dp = ("z8", "z0", "core")
    in_specs = (P(dp, "shard", None), P(dp, "shard", None), P("shard", None))
    out_specs = (P(dp, "shard", None), P("shard", None))
    return jax.shard_map(
        per_device, mesh=parts, in_specs=in_specs, out_specs=out_specs, check_vma=False
    )
```

```python
import functools

import jax
import jax.numpy as jnp
from jax import lax
from jax.experimental import pallas as pl
from jax.experimental.pallas import tpu as pltpu
from jax.sharding import Mesh, PartitionSpec as P

F32, BF16 = jnp.float32, jnp.bfloat16
HIGH = lax.Precision.HIGHEST
PLANE = ("z0", "shard")
SWAP = [(0, 1), (1, 0)]
VMEM = pl.BlockSpec(memory_space=pltpu.VMEM)
ANY = pl.BlockSpec(memory_space=pl.ANY)
CUTS = 7
STRIDE = 4
SMEM = pl.BlockSpec(memory_space=pltpu.SMEM)


def call(body, out, operands, specs, scratch=(), out_specs=None, flops=0, limit=24):
    moved = sum(o.size * o.dtype.itemsize for o in [*operands, *out])
    return pl.pallas_call(
        body,
        out_shape=out,
        in_specs=specs,
        out_specs=out_specs or [VMEM] * len(out),
        scratch_shapes=list(scratch),
        compiler_params=pltpu.CompilerParams(vmem_limit_bytes=limit * 2**20),
        cost_estimate=pl.CostEstimate(flops=flops, bytes_accessed=moved, transcendentals=0),
    )(*operands)


def split(x, parts):
    out = []
    for _ in range(parts):
        part = x.astype(BF16)
        out.append(part)
        x = x - part.astype(F32)
    return out


def dot(a, b, dims, precision=None):
    return lax.dot_general(a, b, (dims, ((), ())), precision=precision, preferred_element_type=F32)


def ask_kernel(place_ref, q_ref, out_ref):
    half = q_ref.shape[0] // 2
    mine = q_ref[pl.ds(pl.multiple_of(place_ref[0] * half, half), half), :]
    packed = jnp.concatenate([mine[: half // 2], mine[half // 2 :]], axis=1)
    out_ref[...] = jnp.broadcast_to(packed[None], out_ref.shape)


def line_kernel(q_ref, out_ref):
    shards, low, span = q_ref.shape
    share = span // 2
    for g in range(shards // 2):
        a, b = q_ref[2 * g], q_ref[2 * g + 1]
        pair = jnp.concatenate(
            [
                jnp.concatenate([a[:, :share], b[:, :share]], axis=1),
                jnp.concatenate([a[:, share:], b[:, share:]], axis=1),
            ],
            axis=0,
        )
        for i, part in enumerate(split(pair, 2)):
            out_ref[2 * low * i : 2 * low * (i + 1), span * g : span * (g + 1)] = part


def left_kernel(q_ref, own_ref, other_ref, parts_ref, out_ref, other_buf, sem):
    half = q_ref.shape[0] // 2
    rows, width = own_ref.shape
    step = width // CUTS
    cuts = [slice(g * step, (g + 1) * step) for g in range(CUTS)]
    loads = []
    for g, cols in enumerate(cuts):
        loads.append(pltpu.make_async_copy(other_ref.at[:, cols], other_buf.at[:, cols], sem.at[g]))
        loads[-1].start()
    total = jnp.zeros((2 * half, 2 * rows), F32)
    for g, cols in enumerate(cuts):
        loads[g].wait()
        for i, part in enumerate(split(own_ref[:, cols] + other_buf[:, cols], 2)):
            parts_ref[i * rows : (i + 1) * rows, cols] = part
        total = total + dot(q_ref[:, cols], parts_ref[:, cols], ((1,), (1,)))
    left = total[half:, rows:] + total[half:, :rows] + total[:half, rows:]
    left = left + total[:half, :rows]
    packed = jnp.concatenate([left[: half // 2], left[half // 2 :]], axis=1)
    out_ref[...] = jnp.broadcast_to(packed[None], out_ref.shape)


def right_kernel(replicas, place_ref, left_ref, parts_ref, out_ref, mine_ref):
    width = parts_ref.shape[1]
    step = width // 8
    quarter = left_ref.shape[1] // 2
    packed = left_ref[0]
    for z in range(1, left_ref.shape[0]):
        packed = packed + left_ref[z]
    packed = packed * (1.0 / replicas)
    rows = packed.shape[1] // 2
    half = 2 * packed.shape[0]
    left = jnp.concatenate([packed[:, :rows], packed[:, rows:]], axis=0)
    mine_ref[...] = left
    big, low = (part.astype(F32) for part in split(left, 2))
    stacked = jnp.concatenate(
        [jnp.concatenate([big, big], axis=1), jnp.concatenate([low, low], axis=1)], axis=0
    ).astype(BF16)
    mine = jnp.where(place_ref[2] == 0, left[: half // 2], left[half // 2 :])
    mine = jnp.concatenate([mine[:quarter], mine[quarter:]], axis=1)
    for g in range(8):
        product = dot(stacked, parts_ref[:, g * step : (g + 1) * step], ((1,), (0,)))
        right = (product[half:] + product[:half]) * (1.0 / replicas)
        for z in range(2):
            for k in range(2):
                row = quarter * (2 * z + k)
                out_ref[z, 2 * g + k] = jnp.concatenate([right[row : row + quarter], mine], axis=1)


def scatter_kernel(got_ref, out_ref, left_ref):
    quarter, span = out_ref.shape[1:]
    rows = (got_ref.shape[3] - span) // 2
    total = got_ref[0, 0, :, :span]
    for s in range(1, got_ref.shape[1]):
        total = total + got_ref[0, s, :, :span]
    for s in range(got_ref.shape[1]):
        total = total + got_ref[1, s, :, :span]
    out_ref[...] = jnp.broadcast_to(total[None], out_ref.shape)
    for z in range(2):
        for g in range(got_ref.shape[1] // 2):
            a, b = got_ref[z, 2 * g, :, span:], got_ref[z, 2 * g + 1, :, span:]
            eight = jnp.concatenate(
                [
                    jnp.concatenate([a[:, :rows], b[:, :rows]], axis=1),
                    jnp.concatenate([a[:, rows:], b[:, rows:]], axis=1),
                ],
                axis=0,
            )
            left_ref[2 * quarter * z : 2 * quarter * (z + 1), 2 * rows * g : 2 * rows * (g + 1)] = eight


def spread_kernel(got_ref, weights_ref, inverse_ref, out_ref):
    total = got_ref[0]
    for z in range(1, got_ref.shape[0]):
        total = total + got_ref[z]
    out_ref[...] = jnp.broadcast_to(total[None], out_ref.shape)


def factor_kernel(place_ref, own_ref, other_ref, mine_ref, weights_ref, inverse_ref, left_ref, both_ref):
    core, here = place_ref[0], place_ref[1]
    half, rows = mine_ref.shape
    rank = 2 * half
    first = pl.ds(pl.multiple_of(core * half, half), half)
    second = pl.ds(pl.multiple_of((1 - core) * half, half), half)
    left_ref[first, :] = own_ref[...]
    left_ref[second, :] = other_ref[...]
    pair = other_ref[:, pl.ds(pl.multiple_of(here // 2 * 2 * rows, 2 * rows), 2 * rows)]
    both_ref[first, :] = mine_ref[...]
    both_ref[second, :] = jnp.where(here % 2 == 0, pair[:, :rows], pair[:, rows:])
    parts = jnp.concatenate(split(left_ref[...], 3), axis=0)
    products = dot(parts, parts, ((1,), (1,)))
    block = lambda i, j: products[i * rank : (i + 1) * rank, j * rank : (j + 1) * rank]
    gram = block(2, 0) + block(1, 1) + block(0, 2)
    gram = gram + (block(1, 0) + block(0, 1))
    gram = gram + block(0, 0)
    at_row = lax.broadcasted_iota(jnp.int32, (rank, 4 * rank), 0)
    at_lane = lax.broadcasted_iota(jnp.int32, (rank, 4 * rank), 1)
    work = jnp.concatenate([gram, jnp.zeros((rank, rank), F32), both_ref[...]], axis=1)
    work = jnp.where(at_lane == at_row + rank, 1.0, work)
    for start in range(0, rank, STRIDE):
        columns = [jnp.broadcast_to(work[:, j : j + 1], work.shape) for j in range(start, start + STRIDE)]
        for t in range(STRIDE):
            j = start + t
            factor = jnp.where(at_row > j, columns[t] * (1.0 / columns[t][j : j + 1]), 0.0)
            for u in range(t + 1, STRIDE):
                columns[u] = columns[u] - factor * columns[u][j : j + 1]
            work = work - factor * work[j : j + 1]
    pivots = jnp.sum(jnp.where(at_lane == at_row, work, 0.0), axis=1, keepdims=True)
    work = work / jnp.sqrt(pivots)
    inverse = work[:, rank : 2 * rank]
    mine = dot(work[:, 2 * rank :], inverse, ((0,), (0,)), HIGH)
    big, low = (part.astype(F32) for part in split(mine, 2))
    weights_ref[...] = jnp.concatenate(
        [jnp.concatenate([big, big], axis=1), jnp.concatenate([low, low], axis=1)], axis=0
    ).astype(BF16)
    inverse_ref[...] = inverse


def final_kernel(place_ref, raw_ref, weights_ref, inverse_ref, merged_ref, out_ref, q_ref, hold_ref, sem):
    here = place_ref[1]
    rows, width = hold_ref.shape
    step = raw_ref.shape[-1]
    gather = lambda g: jnp.concatenate(
        [raw_ref[core, z, 2 * g + k] for core in range(2) for z in range(2) for k in range(2)], axis=0
    )
    copies = []
    for g in range(width // step):
        cols = slice(g * step, (g + 1) * step)
        product = dot(weights_ref[...], jnp.concatenate(split(gather(g), 2), axis=0), ((1,), (0,)))
        hold_ref[:, cols] = merged_ref[:, cols] - (product[rows:] + product[:rows])
        copy = pltpu.make_async_copy(hold_ref.at[:, cols], out_ref.at[:, cols], sem.at[g])
        copy.start()
        copies.append(copy)
    raw = gather(here // 2)
    raw = jnp.where(here % 2 == 0, raw[:, : step // 2], raw[:, step // 2 :])
    q_ref[...] = dot(inverse_ref[...], raw, ((1,), (0,)), HIGH)
    for copy in copies:
        copy.wait()


def per_device(grads, errors, q_prev):
    shape = jax.ShapeDtypeStruct
    rows, width = errors.shape[1:]
    share, rank = q_prev.shape
    half = rank // 2
    place = jnp.stack([lax.axis_index(axis) for axis in ("core", "shard", "z0")])
    replicas = 32

    (own_q,) = call(
        ask_kernel,
        [shape((16, half // 2, 2 * share), F32)],
        [place, q_prev.T],
        [SMEM, VMEM],
    )
    all_q = lax.all_to_all(own_q, "shard", 0, 0)
    merged = grads[0].astype(F32) + errors[0]
    other = lax.ppermute(merged, "core", SWAP)
    (all_q,) = call(
        line_kernel,
        [shape((2 * half, width), BF16)],
        [all_q],
        [VMEM],
        flops=10**11,
    )
    parts, left = call(
        left_kernel,
        [shape((2 * rows, width), BF16), shape((16, 8, 128), F32)],
        [all_q, merged, other],
        [VMEM, VMEM, ANY],
        [pltpu.VMEM((rows, width), F32), pltpu.SemaphoreType.DMA((CUTS,))],
        flops=2 * 32 * 128 * width,
    )
    left = lax.all_to_all(left, ("z8", "z0"), 0, 0)

    pieces, mine = call(
        functools.partial(right_kernel, replicas),
        [shape((2, 16, half // 4, 1024), F32), shape((half, rows), F32)],
        [place, left, parts],
        [SMEM, VMEM, VMEM],
        flops=2 * 32 * 128 * width,
    )
    pieces = lax.all_to_all(pieces.reshape(32, half // 4, 1024), PLANE, 0, 0).reshape(pieces.shape)
    right, left_own = call(
        scatter_kernel,
        [shape((8, half // 4, 2 * share), F32), shape((half, 16 * rows), F32)],
        [pieces],
        [VMEM],
    )
    right = lax.all_to_all(right, "z8", 0, 0)

    left_other = lax.ppermute(left_own, "core", SWAP)
    weights, inverse = call(
        factor_kernel,
        [shape((2 * rows, 2 * rank), BF16), shape((rank, rank), F32)],
        [place, left_own, left_other, mine],
        [SMEM] + [VMEM] * 3,
        [pltpu.VMEM((rank, 16 * rows), F32), pltpu.VMEM((rank, rows), F32)],
        flops=10**7,
    )

    (raw,) = call(
        spread_kernel, [shape((32, half // 4, 2 * share), F32)], [right, weights, inverse], [VMEM] * 3
    )
    raw = lax.all_to_all(raw, PLANE, 0, 0)
    raw = lax.all_gather(raw, "core").reshape(2, 2, 16, half // 4, 2 * share)
    out, q_new = call(
        final_kernel,
        [shape((rows, width), F32), shape((rank, share), F32)],
        [place, raw, weights, inverse, merged],
        [SMEM] + [VMEM] * 4,
        [pltpu.VMEM((rows, width), F32), pltpu.SemaphoreType.DMA((8,))],
        [pl.BlockSpec(memory_space=pl.ANY), VMEM],
        flops=2 * 128 * 64 * width,
    )
    return (out[None], q_new.T)


def solution(mesh):
    parts = Mesh(mesh.devices.reshape(8, 2, 2, 16), ("z8", "z0", "core", "shard"))
    dp = ("z8", "z0", "core")
    in_specs = (P(dp, "shard", None), P(dp, "shard", None), P("shard", None))
    out_specs = (P(dp, "shard", None), P("shard", None))
    return jax.shard_map(
        per_device, mesh=parts, in_specs=in_specs, out_specs=out_specs, check_vma=False
    )
```

```python
import functools

import jax
import jax.numpy as jnp
from jax import lax
from jax.experimental import pallas as pl
from jax.experimental.pallas import tpu as pltpu
from jax.sharding import Mesh, PartitionSpec as P

F32, BF16 = jnp.float32, jnp.bfloat16
HIGH = lax.Precision.HIGHEST
PLANE = ("z0", "shard")
SWAP = [(0, 1), (1, 0)]
VMEM = pl.BlockSpec(memory_space=pltpu.VMEM)
ANY = pl.BlockSpec(memory_space=pl.ANY)
CUTS = 7
STRIDE = 4
SMEM = pl.BlockSpec(memory_space=pltpu.SMEM)


ASKED = 10
FIRST = 10
START = 11
TURN = 5


def place_of(peer, first=FIRST):
    return first if peer == 0 else 0 if peer == first else peer


def exchange(blocks, axis, order):
    return lax.all_to_all(blocks, axis, 0, 0, axis_index_groups=[list(order)])


def call(body, out, operands, specs, scratch=(), out_specs=None, flops=0, limit=24):
    moved = sum(o.size * o.dtype.itemsize for o in [*operands, *out])
    return pl.pallas_call(
        body,
        out_shape=out,
        in_specs=specs,
        out_specs=out_specs or [VMEM] * len(out),
        scratch_shapes=list(scratch),
        compiler_params=pltpu.CompilerParams(vmem_limit_bytes=limit * 2**20),
        cost_estimate=pl.CostEstimate(flops=flops, bytes_accessed=moved, transcendentals=0),
    )(*operands)


def split(x, parts):
    out = []
    for _ in range(parts):
        part = x.astype(BF16)
        out.append(part)
        x = x - part.astype(F32)
    return out


def dot(a, b, dims, precision=None):
    return lax.dot_general(a, b, (dims, ((), ())), precision=precision, preferred_element_type=F32)


def ask_kernel(place_ref, q_ref, out_ref):
    half = q_ref.shape[0] // 2
    mine = q_ref[pl.ds(pl.multiple_of(place_ref[0] * half, half), half), :]
    packed = jnp.concatenate([mine[: half // 2], mine[half // 2 :]], axis=1)
    out_ref[...] = jnp.broadcast_to(packed[None], out_ref.shape)


def line_kernel(q_ref, out_ref):
    shards, low, span = q_ref.shape
    share = span // 2
    for g in range(shards // 2):
        a, b = q_ref[place_of(2 * g, ASKED)], q_ref[place_of(2 * g + 1, ASKED)]
        pair = jnp.concatenate(
            [
                jnp.concatenate([a[:, :share], b[:, :share]], axis=1),
                jnp.concatenate([a[:, share:], b[:, share:]], axis=1),
            ],
            axis=0,
        )
        for i, part in enumerate(split(pair, 2)):
            out_ref[2 * low * i : 2 * low * (i + 1), span * g : span * (g + 1)] = part


def left_kernel(q_ref, own_ref, other_ref, parts_ref, out_ref, other_buf, sem):
    half = q_ref.shape[0] // 2
    rows, width = own_ref.shape
    step = width // CUTS
    cuts = [slice(g * step, (g + 1) * step) for g in range(CUTS)]
    loads = []
    for g, cols in enumerate(cuts):
        loads.append(pltpu.make_async_copy(other_ref.at[:, cols], other_buf.at[:, cols], sem.at[g]))
        loads[-1].start()
    total = jnp.zeros((2 * half, 2 * rows), F32)
    for g, cols in enumerate(cuts):
        loads[g].wait()
        for i, part in enumerate(split(own_ref[:, cols] + other_buf[:, cols], 2)):
            parts_ref[i * rows : (i + 1) * rows, cols] = part
        total = total + dot(q_ref[:, cols], parts_ref[:, cols], ((1,), (1,)))
    left = total[half:, rows:] + total[half:, :rows] + total[:half, rows:]
    left = left + total[:half, :rows]
    packed = jnp.concatenate([left[: half // 2], left[half // 2 :]], axis=1)
    out_ref[...] = jnp.broadcast_to(packed[None], out_ref.shape)


def right_kernel(replicas, place_ref, left_ref, parts_ref, out_ref, mine_ref):
    width = parts_ref.shape[1]
    step = width // 8
    quarter = left_ref.shape[1] // 2
    packed = left_ref[0]
    for z in range(1, left_ref.shape[0]):
        packed = packed + left_ref[z]
    packed = packed * (1.0 / replicas)
    rows = packed.shape[1] // 2
    half = 2 * packed.shape[0]
    left = jnp.concatenate([packed[:, :rows], packed[:, rows:]], axis=0)
    mine_ref[...] = left
    big, low = (part.astype(F32) for part in split(left, 2))
    stacked = jnp.concatenate(
        [jnp.concatenate([big, big], axis=1), jnp.concatenate([low, low], axis=1)], axis=0
    ).astype(BF16)
    mine = jnp.where(place_ref[2] == 0, left[: half // 2], left[half // 2 :])
    mine = jnp.concatenate([mine[:quarter], mine[quarter:]], axis=1)
    for g in range(8):
        product = dot(stacked, parts_ref[:, g * step : (g + 1) * step], ((1,), (0,)))
        right = (product[half:] + product[:half]) * (1.0 / replicas)
        for z in range(2):
            for k in range(2):
                row = quarter * (2 * z + k)
                out_ref[place_of(16 * z + 2 * g + k)] = jnp.concatenate([right[row : row + quarter], mine], axis=1)


def scatter_kernel(got_ref, out_ref, left_ref):
    quarter, span = out_ref.shape[1:]
    peers = got_ref.shape[0]
    rows = (got_ref.shape[2] - span) // 2
    total = got_ref[0, :, :span]
    for peer in range(1, peers):
        total = total + got_ref[peer, :, :span]
    out_ref[...] = jnp.broadcast_to(total[None], out_ref.shape)
    for z in range(2):
        for g in range(peers // 4):
            a, b = (got_ref[place_of(peers // 2 * z + 2 * g + k), :, span:] for k in range(2))
            eight = jnp.concatenate(
                [
                    jnp.concatenate([a[:, :rows], b[:, :rows]], axis=1),
                    jnp.concatenate([a[:, rows:], b[:, rows:]], axis=1),
                ],
                axis=0,
            )
            left_ref[2 * quarter * z : 2 * quarter * (z + 1), 2 * rows * g : 2 * rows * (g + 1)] = eight


def spread_kernel(got_ref, weights_ref, inverse_ref, out_ref):
    total = got_ref[0]
    for z in range(1, got_ref.shape[0]):
        total = total + got_ref[z]
    out_ref[...] = jnp.broadcast_to(total[None], out_ref.shape)


def factor_kernel(place_ref, own_ref, other_ref, mine_ref, weights_ref, inverse_ref, left_ref, both_ref):
    core, here = place_ref[0], place_ref[1]
    half, rows = mine_ref.shape
    rank = 2 * half
    first = pl.ds(pl.multiple_of(core * half, half), half)
    second = pl.ds(pl.multiple_of((1 - core) * half, half), half)
    left_ref[first, :] = own_ref[...]
    left_ref[second, :] = other_ref[...]
    pair = other_ref[:, pl.ds(pl.multiple_of(here // 2 * 2 * rows, 2 * rows), 2 * rows)]
    both_ref[first, :] = mine_ref[...]
    both_ref[second, :] = jnp.where(here % 2 == 0, pair[:, :rows], pair[:, rows:])
    parts = jnp.concatenate(split(left_ref[...], 3), axis=0)
    products = dot(parts, parts, ((1,), (1,)))
    block = lambda i, j: products[i * rank : (i + 1) * rank, j * rank : (j + 1) * rank]
    gram = block(2, 0) + block(1, 1) + block(0, 2)
    gram = gram + (block(1, 0) + block(0, 1))
    gram = gram + block(0, 0)
    at_row = lax.broadcasted_iota(jnp.int32, (rank, 4 * rank), 0)
    at_lane = lax.broadcasted_iota(jnp.int32, (rank, 4 * rank), 1)
    work = jnp.concatenate([gram, jnp.zeros((rank, rank), F32), both_ref[...]], axis=1)
    work = jnp.where(at_lane == at_row + rank, 1.0, work)
    for start in range(0, rank, STRIDE):
        columns = [jnp.broadcast_to(work[:, j : j + 1], work.shape) for j in range(start, start + STRIDE)]
        for t in range(STRIDE):
            j = start + t
            factor = jnp.where(at_row > j, columns[t] * (1.0 / columns[t][j : j + 1]), 0.0)
            for u in range(t + 1, STRIDE):
                columns[u] = columns[u] - factor * columns[u][j : j + 1]
            work = work - factor * work[j : j + 1]
    pivots = jnp.sum(jnp.where(at_lane == at_row, work, 0.0), axis=1, keepdims=True)
    work = work / jnp.sqrt(pivots)
    inverse = work[:, rank : 2 * rank]
    mine = dot(work[:, 2 * rank :], inverse, ((0,), (0,)), HIGH)
    big, low = (part.astype(F32) for part in split(mine, 2))
    weights_ref[...] = jnp.concatenate(
        [jnp.concatenate([big, big], axis=1), jnp.concatenate([low, low], axis=1)], axis=0
    ).astype(BF16)
    inverse_ref[...] = inverse


def final_kernel(place_ref, raw_ref, weights_ref, inverse_ref, merged_ref, out_ref, q_ref, hold_ref, sem):
    here = place_ref[1]
    rows, width = hold_ref.shape
    step = raw_ref.shape[-1]
    gather = lambda peers: jnp.concatenate([raw_ref[core, peer] for core in range(2) for peer in peers], axis=0)
    copies = []
    for g in range(width // step):
        cols = slice(g * step, (g + 1) * step)
        product = dot(weights_ref[...], jnp.concatenate(split(gather([place_of(16 * z + 2 * g + k) for z in range(2) for k in range(2)]), 2), axis=0), ((1,), (0,)))
        hold_ref[:, cols] = merged_ref[:, cols] - (product[rows:] + product[:rows])
        copy = pltpu.make_async_copy(hold_ref.at[:, cols], out_ref.at[:, cols], sem.at[g])
        copy.start()
        copies.append(copy)
    peers = [here // 2 * 2 + 16 * z + k for z in range(2) for k in range(2)]
    raw = gather([jnp.where(peer == 0, FIRST, jnp.where(peer == FIRST, 0, peer)) for peer in peers])
    raw = jnp.where(here % 2 == 0, raw[:, : step // 2], raw[:, step // 2 :])
    q_ref[...] = dot(inverse_ref[...], raw, ((1,), (0,)), HIGH)
    for copy in copies:
        copy.wait()


def per_device(grads, errors, q_prev):
    shape = jax.ShapeDtypeStruct
    rows, width = errors.shape[1:]
    share, rank = q_prev.shape
    half = rank // 2
    place = jnp.stack([lax.axis_index(axis) for axis in ("core", "shard", "z0")])
    replicas = 32

    (own_q,) = call(
        ask_kernel,
        [shape((16, half // 2, 2 * share), F32)],
        [place, q_prev.T],
        [SMEM, VMEM],
    )
    all_q = exchange(own_q, "shard", (place_of(s, ASKED) for s in range(16)))
    merged = grads[0].astype(F32) + errors[0]
    other = lax.ppermute(merged, "core", SWAP)
    (all_q,) = call(
        line_kernel,
        [shape((2 * half, width), BF16)],
        [all_q],
        [VMEM],
        flops=10**11,
    )
    parts, left = call(
        left_kernel,
        [shape((2 * rows, width), BF16), shape((16, 8, 128), F32)],
        [all_q, merged, other],
        [VMEM, VMEM, ANY],
        [pltpu.VMEM((rows, width), F32), pltpu.SemaphoreType.DMA((CUTS,))],
        flops=2 * 32 * 128 * width,
    )
    left = exchange(left, ("z8", "z0"), ((z + START) % 16 for z in range(16)))

    pieces, mine = call(
        functools.partial(right_kernel, replicas),
        [shape((32, half // 4, 1024), F32), shape((half, rows), F32)],
        [place, left, parts],
        [SMEM, VMEM, VMEM],
        flops=2 * 32 * 128 * width,
    )
    pieces = exchange(pieces, PLANE, map(place_of, range(32)))
    right, left_own = call(
        scatter_kernel,
        [shape((8, half // 4, 2 * share), F32), shape((half, 16 * rows), F32)],
        [pieces],
        [VMEM],
    )
    right = exchange(right, "z8", ((z + TURN) % 8 for z in range(8)))

    left_other = lax.ppermute(left_own, "core", SWAP)
    weights, inverse = call(
        factor_kernel,
        [shape((2 * rows, 2 * rank), BF16), shape((rank, rank), F32)],
        [place, left_own, left_other, mine],
        [SMEM] + [VMEM] * 3,
        [pltpu.VMEM((rank, 16 * rows), F32), pltpu.VMEM((rank, rows), F32)],
        flops=10**7,
    )

    (raw,) = call(
        spread_kernel, [shape((32, half // 4, 2 * share), F32)], [right, weights, inverse], [VMEM] * 3
    )
    raw = exchange(raw, PLANE, map(place_of, range(32)))
    raw = lax.all_gather(raw, "core")
    out, q_new = call(
        final_kernel,
        [shape((rows, width), F32), shape((rank, share), F32)],
        [place, raw, weights, inverse, merged],
        [SMEM] + [VMEM] * 4,
        [pltpu.VMEM((rows, width), F32), pltpu.SemaphoreType.DMA((8,))],
        [pl.BlockSpec(memory_space=pl.ANY), VMEM],
        flops=2 * 128 * 64 * width,
    )
    return (out[None], q_new.T)


def solution(mesh):
    parts = Mesh(mesh.devices.reshape(8, 2, 2, 16), ("z8", "z0", "core", "shard"))
    dp = ("z8", "z0", "core")
    in_specs = (P(dp, "shard", None), P(dp, "shard", None), P("shard", None))
    out_specs = (P(dp, "shard", None), P("shard", None))
    return jax.shard_map(
        per_device, mesh=parts, in_specs=in_specs, out_specs=out_specs, check_vma=False
    )
```

```python
import functools

import jax
import jax.numpy as jnp
from jax import lax
from jax.experimental import pallas as pl
from jax.experimental.pallas import tpu as pltpu
from jax.sharding import Mesh, PartitionSpec as P

F32, BF16 = jnp.float32, jnp.bfloat16
HIGH = lax.Precision.HIGHEST
PLANE = ("z0", "shard")
SWAP = [(0, 1), (1, 0)]
VMEM = pl.BlockSpec(memory_space=pltpu.VMEM)
ANY = pl.BlockSpec(memory_space=pl.ANY)
CUTS = 7
STRIDE = 4


ASKED = 10
FIRST = 10
START = 11
TURN = 5


def place_of(peer, first=FIRST):
    return first if peer == 0 else 0 if peer == first else peer


def exchange(blocks, axis, order):
    return lax.all_to_all(blocks, axis, 0, 0, axis_index_groups=[list(order)])


def call(body, out, operands, specs, scratch=(), out_specs=None, flops=0, limit=24):
    moved = sum(o.size * o.dtype.itemsize for o in [*operands, *out])
    return pl.pallas_call(
        body,
        out_shape=out,
        in_specs=specs,
        out_specs=out_specs or [VMEM] * len(out),
        scratch_shapes=list(scratch),
        compiler_params=pltpu.CompilerParams(vmem_limit_bytes=limit * 2**20),
        cost_estimate=pl.CostEstimate(flops=flops, bytes_accessed=moved, transcendentals=0),
    )(*operands)


def split(x, parts):
    out = []
    for _ in range(parts):
        part = x.astype(BF16)
        out.append(part)
        x = x - part.astype(F32)
    return out


def dot(a, b, dims, precision=None):
    return lax.dot_general(a, b, (dims, ((), ())), precision=precision, preferred_element_type=F32)


def ask_kernel(q_ref, out_ref):
    half = q_ref.shape[0] // 2
    mine = q_ref[pl.ds(pl.multiple_of(lax.axis_index("core") * half, half), half), :]
    packed = jnp.concatenate([mine[: half // 2], mine[half // 2 :]], axis=1)
    out_ref[...] = jnp.broadcast_to(packed[None], out_ref.shape)


def line_kernel(q_ref, out_ref):
    shards, low, span = q_ref.shape
    share = span // 2
    for g in range(shards // 2):
        a, b = q_ref[place_of(2 * g, ASKED)], q_ref[place_of(2 * g + 1, ASKED)]
        pair = jnp.concatenate(
            [
                jnp.concatenate([a[:, :share], b[:, :share]], axis=1),
                jnp.concatenate([a[:, share:], b[:, share:]], axis=1),
            ],
            axis=0,
        )
        for i, part in enumerate(split(pair, 2)):
            out_ref[2 * low * i : 2 * low * (i + 1), span * g : span * (g + 1)] = part


def left_kernel(q_ref, own_ref, other_ref, parts_ref, out_ref, other_buf, sem):
    half = q_ref.shape[0] // 2
    rows, width = own_ref.shape
    step = width // CUTS
    cuts = [slice(g * step, (g + 1) * step) for g in range(CUTS)]
    loads = []
    for g, cols in enumerate(cuts):
        loads.append(pltpu.make_async_copy(other_ref.at[:, cols], other_buf.at[:, cols], sem.at[g]))
        loads[-1].start()
    total = jnp.zeros((2 * half, 2 * rows), F32)
    for g, cols in enumerate(cuts):
        loads[g].wait()
        for i, part in enumerate(split(own_ref[:, cols] + other_buf[:, cols], 2)):
            parts_ref[i * rows : (i + 1) * rows, cols] = part
        total = total + dot(q_ref[:, cols], parts_ref[:, cols], ((1,), (1,)))
    left = total[half:, rows:] + total[half:, :rows] + total[:half, rows:]
    left = left + total[:half, :rows]
    packed = jnp.concatenate([left[: half // 2], left[half // 2 :]], axis=1)
    out_ref[...] = jnp.broadcast_to(packed[None], out_ref.shape)


def right_kernel(replicas, left_ref, parts_ref, out_ref, mine_ref):
    width = parts_ref.shape[1]
    step = width // 8
    quarter = left_ref.shape[1] // 2
    packed = left_ref[0]
    for z in range(1, left_ref.shape[0]):
        packed = packed + left_ref[z]
    packed = packed * (1.0 / replicas)
    rows = packed.shape[1] // 2
    half = 2 * packed.shape[0]
    left = jnp.concatenate([packed[:, :rows], packed[:, rows:]], axis=0)
    mine_ref[...] = left
    big, low = (part.astype(F32) for part in split(left, 2))
    stacked = jnp.concatenate(
        [jnp.concatenate([big, big], axis=1), jnp.concatenate([low, low], axis=1)], axis=0
    ).astype(BF16)
    mine = jnp.where(lax.axis_index("z0") == 0, left[: half // 2], left[half // 2 :])
    mine = jnp.concatenate([mine[:quarter], mine[quarter:]], axis=1)
    for g in range(8):
        product = dot(stacked, parts_ref[:, g * step : (g + 1) * step], ((1,), (0,)))
        right = (product[half:] + product[:half]) * (1.0 / replicas)
        for z in range(2):
            for k in range(2):
                row = quarter * (2 * z + k)
                out_ref[place_of(16 * z + 2 * g + k)] = jnp.concatenate([right[row : row + quarter], mine], axis=1)


def scatter_kernel(got_ref, out_ref, left_ref):
    quarter, span = out_ref.shape[1:]
    peers = got_ref.shape[0]
    rows = (got_ref.shape[2] - span) // 2
    total = got_ref[0, :, :span]
    for peer in range(1, peers):
        total = total + got_ref[peer, :, :span]
    out_ref[...] = jnp.broadcast_to(total[None], out_ref.shape)
    for z in range(2):
        for g in range(peers // 4):
            a, b = (got_ref[place_of(peers // 2 * z + 2 * g + k), :, span:] for k in range(2))
            eight = jnp.concatenate(
                [
                    jnp.concatenate([a[:, :rows], b[:, :rows]], axis=1),
                    jnp.concatenate([a[:, rows:], b[:, rows:]], axis=1),
                ],
                axis=0,
            )
            left_ref[2 * quarter * z : 2 * quarter * (z + 1), 2 * rows * g : 2 * rows * (g + 1)] = eight


def spread_kernel(got_ref, weights_ref, inverse_ref, out_ref):
    total = got_ref[0]
    for z in range(1, got_ref.shape[0]):
        total = total + got_ref[z]
    out_ref[...] = jnp.broadcast_to(total[None], out_ref.shape)


def factor_kernel(own_ref, other_ref, mine_ref, weights_ref, inverse_ref, left_ref, both_ref):
    core, here = lax.axis_index("core"), lax.axis_index("shard")
    half, rows = mine_ref.shape
    rank = 2 * half
    first = pl.ds(pl.multiple_of(core * half, half), half)
    second = pl.ds(pl.multiple_of((1 - core) * half, half), half)
    left_ref[first, :] = own_ref[...]
    left_ref[second, :] = other_ref[...]
    pair = other_ref[:, pl.ds(pl.multiple_of(here // 2 * 2 * rows, 2 * rows), 2 * rows)]
    both_ref[first, :] = mine_ref[...]
    both_ref[second, :] = jnp.where(here % 2 == 0, pair[:, :rows], pair[:, rows:])
    parts = jnp.concatenate(split(left_ref[...], 3), axis=0)
    products = dot(parts, parts, ((1,), (1,)))
    block = lambda i, j: products[i * rank : (i + 1) * rank, j * rank : (j + 1) * rank]
    gram = block(2, 0) + block(1, 1) + block(0, 2)
    gram = gram + (block(1, 0) + block(0, 1))
    gram = gram + block(0, 0)
    at_row = lax.broadcasted_iota(jnp.int32, (rank, 4 * rank), 0)
    at_lane = lax.broadcasted_iota(jnp.int32, (rank, 4 * rank), 1)
    work = jnp.concatenate([gram, jnp.zeros((rank, rank), F32), both_ref[...]], axis=1)
    work = jnp.where(at_lane == at_row + rank, 1.0, work)
    for start in range(0, rank, STRIDE):
        columns = [jnp.broadcast_to(work[:, j : j + 1], work.shape) for j in range(start, start + STRIDE)]
        for t in range(STRIDE):
            j = start + t
            factor = jnp.where(at_row > j, columns[t] * (1.0 / columns[t][j : j + 1]), 0.0)
            for u in range(t + 1, STRIDE):
                columns[u] = columns[u] - factor * columns[u][j : j + 1]
            work = work - factor * work[j : j + 1]
    pivots = jnp.sum(jnp.where(at_lane == at_row, work, 0.0), axis=1, keepdims=True)
    work = work / jnp.sqrt(pivots)
    inverse = work[:, rank : 2 * rank]
    mine = dot(work[:, 2 * rank :], inverse, ((0,), (0,)), HIGH)
    big, low = (part.astype(F32) for part in split(mine, 2))
    weights_ref[...] = jnp.concatenate([big, big, low], axis=1).astype(BF16)
    inverse_ref[...] = inverse


def final_kernel(raw_ref, weights_ref, inverse_ref, merged_ref, out_ref, q_ref, hold_ref, q_buf, sem):
    here = lax.axis_index("shard")
    width = hold_ref.shape[1]
    step = raw_ref.shape[-1]
    gather = lambda peers: jnp.concatenate([raw_ref[core, peer] for core in range(2) for peer in peers], axis=0)
    peers = [here // 2 * 2 + 16 * z + k for z in range(2) for k in range(2)]
    raw = gather([jnp.where(peer == 0, FIRST, jnp.where(peer == FIRST, 0, peer)) for peer in peers])
    raw = jnp.where(here % 2 == 0, raw[:, : step // 2], raw[:, step // 2 :])
    q_buf[...] = dot(inverse_ref[...], raw, ((1,), (0,)), HIGH)
    copies = [pltpu.make_async_copy(q_buf, q_ref, sem.at[width // step])]
    copies[0].start()
    for g in range(width // step):
        cols = slice(g * step, (g + 1) * step)
        big, low = split(gather([place_of(16 * z + 2 * g + k) for z in range(2) for k in range(2)]), 2)
        approx = dot(weights_ref[...], jnp.concatenate([big, low, big], axis=0), ((1,), (0,)))
        hold_ref[:, cols] = merged_ref[:, cols] - approx
        copy = pltpu.make_async_copy(hold_ref.at[:, cols], out_ref.at[:, cols], sem.at[g])
        copy.start()
        copies.append(copy)
    for copy in copies:
        copy.wait()


def per_device(grads, errors, q_prev):
    shape = jax.ShapeDtypeStruct
    rows, width = errors.shape[1:]
    share, rank = q_prev.shape
    half = rank // 2
    replicas = 32

    (own_q,) = call(
        ask_kernel,
        [shape((16, half // 2, 2 * share), F32)],
        [q_prev.T],
        [VMEM],
    )
    all_q = exchange(own_q, "shard", (place_of(s, ASKED) for s in range(16)))
    merged = grads[0].astype(F32) + errors[0]
    other = lax.ppermute(merged, "core", SWAP)
    (all_q,) = call(
        line_kernel,
        [shape((2 * half, width), BF16)],
        [all_q],
        [VMEM],
        flops=10**11,
    )
    parts, left = call(
        left_kernel,
        [shape((2 * rows, width), BF16), shape((16, 8, 128), F32)],
        [all_q, merged, other],
        [VMEM, VMEM, ANY],
        [pltpu.VMEM((rows, width), F32), pltpu.SemaphoreType.DMA((CUTS,))],
        flops=2 * 32 * 128 * width,
    )
    left = exchange(left, ("z8", "z0"), ((z + START) % 16 for z in range(16)))

    pieces, mine = call(
        functools.partial(right_kernel, replicas),
        [shape((32, half // 4, 1024), F32), shape((half, rows), F32)],
        [left, parts],
        [VMEM, VMEM],
        flops=2 * 32 * 128 * width,
    )
    pieces = exchange(pieces, PLANE, map(place_of, range(32)))
    right, left_own = call(
        scatter_kernel,
        [shape((8, half // 4, 2 * share), F32), shape((half, 16 * rows), F32)],
        [pieces],
        [VMEM],
    )
    right = exchange(right, "z8", ((z + TURN) % 8 for z in range(8)))

    left_other = lax.ppermute(left_own, "core", SWAP)
    weights, inverse = call(
        factor_kernel,
        [shape((rows, 3 * rank), BF16), shape((rank, rank), F32)],
        [left_own, left_other, mine],
        [VMEM] * 3,
        [pltpu.VMEM((rank, 16 * rows), F32), pltpu.VMEM((rank, rows), F32)],
        flops=10**7,
    )

    (raw,) = call(
        spread_kernel, [shape((32, half // 4, 2 * share), F32)], [right, weights, inverse], [VMEM] * 3
    )
    raw = exchange(raw, PLANE, map(place_of, range(32)))
    raw = lax.all_gather(raw, "core")
    out, q_new = call(
        final_kernel,
        [shape((rows, width), F32), shape((rank, share), F32)],
        [raw, weights, inverse, merged],
        [VMEM] * 4,
        [pltpu.VMEM((rows, width), F32), pltpu.VMEM((rank, share), F32), pltpu.SemaphoreType.DMA((9,))],
        [ANY, ANY],
        flops=2 * 96 * 64 * width,
    )
    return (out[None], q_new.T)


def solution(mesh):
    parts = Mesh(mesh.devices.reshape(8, 2, 2, 16), ("z8", "z0", "core", "shard"))
    dp = ("z8", "z0", "core")
    in_specs = (P(dp, "shard", None), P(dp, "shard", None), P("shard", None))
    out_specs = (P(dp, "shard", None), P("shard", None))
    return jax.shard_map(
        per_device, mesh=parts, in_specs=in_specs, out_specs=out_specs, check_vma=False
    )
```

```python
import functools

import jax
import jax.numpy as jnp
from jax import lax
from jax.experimental import pallas as pl
from jax.experimental.pallas import tpu as pltpu
from jax.sharding import Mesh, PartitionSpec as P

F32, BF16 = jnp.float32, jnp.bfloat16
HIGH = lax.Precision.HIGHEST
PLANE = ("z0", "shard")
SWAP = [(0, 1), (1, 0)]
VMEM = pl.BlockSpec(memory_space=pltpu.VMEM)
ANY = pl.BlockSpec(memory_space=pl.ANY)
CUTS = 7
STRIDE = 4


ASKED = 10
FIRST = 10
LEFT_Z = [11, 10, 12, 9, 13, 8, 14, 7, 15, 6, 0, 5, 1, 4, 2, 3]
RIGHT_Z = [10, 12, 14, 0, 2, 4, 6, 8]


def place_of(peer, first=FIRST):
    return 0 if peer == first else peer + (peer < first)


def order_of(peers, first=FIRST):
    return sorted(range(peers), key=lambda peer: place_of(peer, first))


def exchange(blocks, axis, *orders):
    return lax.all_to_all(blocks, axis, 0, 0, axis_index_groups=[list(order) for order in orders])


def call(body, out, operands, specs, scratch=(), out_specs=None, flops=0, limit=24):
    moved = sum(o.size * o.dtype.itemsize for o in [*operands, *out])
    return pl.pallas_call(
        body,
        out_shape=out,
        in_specs=specs,
        out_specs=out_specs or [VMEM] * len(out),
        scratch_shapes=list(scratch),
        compiler_params=pltpu.CompilerParams(vmem_limit_bytes=limit * 2**20),
        cost_estimate=pl.CostEstimate(flops=flops, bytes_accessed=moved, transcendentals=0),
    )(*operands)


def split(x, parts):
    out = []
    for _ in range(parts):
        part = x.astype(BF16)
        out.append(part)
        x = x - part.astype(F32)
    return out


def dot(a, b, dims, precision=None):
    return lax.dot_general(a, b, (dims, ((), ())), precision=precision, preferred_element_type=F32)


def ask_kernel(q_ref, out_ref):
    half = q_ref.shape[0] // 2
    mine = q_ref[pl.ds(pl.multiple_of(lax.axis_index("core") * half, half), half), :]
    packed = jnp.concatenate([mine[: half // 2], mine[half // 2 :]], axis=1)
    out_ref[...] = jnp.broadcast_to(packed[None], out_ref.shape)


def line_kernel(q_ref, out_ref):
    shards, low, span = q_ref.shape
    share = span // 2
    for g in range(shards // 2):
        a, b = q_ref[place_of(2 * g, ASKED)], q_ref[place_of(2 * g + 1, ASKED)]
        pair = jnp.concatenate(
            [
                jnp.concatenate([a[:, :share], b[:, :share]], axis=1),
                jnp.concatenate([a[:, share:], b[:, share:]], axis=1),
            ],
            axis=0,
        )
        for i, part in enumerate(split(pair, 2)):
            out_ref[2 * low * i : 2 * low * (i + 1), span * g : span * (g + 1)] = part


def left_kernel(q_ref, own_ref, other_ref, parts_ref, out_ref, other_buf, sem):
    half = q_ref.shape[0] // 2
    rows, width = own_ref.shape
    step = width // CUTS
    cuts = [slice(g * step, (g + 1) * step) for g in range(CUTS)]
    loads = []
    for g, cols in enumerate(cuts):
        loads.append(pltpu.make_async_copy(other_ref.at[:, cols], other_buf.at[:, cols], sem.at[g]))
        loads[-1].start()
    total = jnp.zeros((2 * half, 2 * rows), F32)
    for g, cols in enumerate(cuts):
        loads[g].wait()
        for i, part in enumerate(split(own_ref[:, cols] + other_buf[:, cols], 2)):
            parts_ref[i * rows : (i + 1) * rows, cols] = part
        total = total + dot(q_ref[:, cols], parts_ref[:, cols], ((1,), (1,)))
    left = total[half:, rows:] + total[half:, :rows] + total[:half, rows:]
    left = left + total[:half, :rows]
    packed = jnp.concatenate([left[: half // 2], left[half // 2 :]], axis=1)
    out_ref[...] = jnp.broadcast_to(packed[None], out_ref.shape)


def right_kernel(replicas, left_ref, parts_ref, out_ref, mine_ref):
    width = parts_ref.shape[1]
    step = width // 8
    quarter = left_ref.shape[1] // 2
    packed = left_ref[0]
    for z in range(1, left_ref.shape[0]):
        packed = packed + left_ref[z]
    packed = packed * (1.0 / replicas)
    rows = packed.shape[1] // 2
    half = 2 * packed.shape[0]
    left = jnp.concatenate([packed[:, :rows], packed[:, rows:]], axis=0)
    mine_ref[...] = left
    big, low = (part.astype(F32) for part in split(left, 2))
    stacked = jnp.concatenate(
        [jnp.concatenate([big, big], axis=1), jnp.concatenate([low, low], axis=1)], axis=0
    ).astype(BF16)
    mine = jnp.where(lax.axis_index("z0") == 0, left[: half // 2], left[half // 2 :])
    mine = jnp.concatenate([mine[:quarter], mine[quarter:]], axis=1)
    for g in range(8):
        product = dot(stacked, parts_ref[:, g * step : (g + 1) * step], ((1,), (0,)))
        right = (product[half:] + product[:half]) * (1.0 / replicas)
        for z in range(2):
            for k in range(2):
                row = quarter * (2 * z + k)
                out_ref[place_of(16 * z + 2 * g + k)] = jnp.concatenate([right[row : row + quarter], mine], axis=1)


def scatter_kernel(got_ref, out_ref, left_ref):
    quarter, span = out_ref.shape[1:]
    peers = got_ref.shape[0]
    rows = (got_ref.shape[2] - span) // 2
    total = got_ref[0, :, :span]
    for peer in range(1, peers):
        total = total + got_ref[peer, :, :span]
    out_ref[...] = jnp.broadcast_to(total[None], out_ref.shape)
    for z in range(2):
        for g in range(peers // 4):
            a, b = (got_ref[place_of(peers // 2 * z + 2 * g + k), :, span:] for k in range(2))
            eight = jnp.concatenate(
                [
                    jnp.concatenate([a[:, :rows], b[:, :rows]], axis=1),
                    jnp.concatenate([a[:, rows:], b[:, rows:]], axis=1),
                ],
                axis=0,
            )
            left_ref[2 * quarter * z : 2 * quarter * (z + 1), 2 * rows * g : 2 * rows * (g + 1)] = eight


def spread_kernel(got_ref, weights_ref, inverse_ref, out_ref):
    total = got_ref[0]
    for z in range(1, got_ref.shape[0]):
        total = total + got_ref[z]
    out_ref[...] = jnp.broadcast_to(total[None], out_ref.shape)


def factor_kernel(own_ref, other_ref, mine_ref, weights_ref, inverse_ref, left_ref, both_ref):
    core, here = lax.axis_index("core"), lax.axis_index("shard")
    half, rows = mine_ref.shape
    rank = 2 * half
    first = pl.ds(pl.multiple_of(core * half, half), half)
    second = pl.ds(pl.multiple_of((1 - core) * half, half), half)
    left_ref[first, :] = own_ref[...]
    left_ref[second, :] = other_ref[...]
    pair = other_ref[:, pl.ds(pl.multiple_of(here // 2 * 2 * rows, 2 * rows), 2 * rows)]
    both_ref[first, :] = mine_ref[...]
    both_ref[second, :] = jnp.where(here % 2 == 0, pair[:, :rows], pair[:, rows:])
    parts = jnp.concatenate(split(left_ref[...], 3), axis=0)
    products = dot(parts, parts, ((1,), (1,)))
    block = lambda i, j: products[i * rank : (i + 1) * rank, j * rank : (j + 1) * rank]
    gram = block(2, 0) + block(1, 1) + block(0, 2)
    gram = gram + (block(1, 0) + block(0, 1))
    gram = gram + block(0, 0)
    at_row = lax.broadcasted_iota(jnp.int32, (rank, 4 * rank), 0)
    at_lane = lax.broadcasted_iota(jnp.int32, (rank, 4 * rank), 1)
    work = jnp.concatenate([gram, jnp.zeros((rank, rank), F32), both_ref[...]], axis=1)
    work = jnp.where(at_lane == at_row + rank, 1.0, work)
    for start in range(0, rank, STRIDE):
        columns = [jnp.broadcast_to(work[:, j : j + 1], work.shape) for j in range(start, start + STRIDE)]
        for t in range(STRIDE):
            j = start + t
            factor = jnp.where(at_row > j, columns[t] * (1.0 / columns[t][j : j + 1]), 0.0)
            for u in range(t + 1, STRIDE):
                columns[u] = columns[u] - factor * columns[u][j : j + 1]
            work = work - factor * work[j : j + 1]
    pivots = jnp.sum(jnp.where(at_lane == at_row, work, 0.0), axis=1, keepdims=True)
    work = work / jnp.sqrt(pivots)
    inverse = work[:, rank : 2 * rank]
    mine = dot(work[:, 2 * rank :], inverse, ((0,), (0,)), HIGH)
    big, low = (part.astype(F32) for part in split(mine, 2))
    weights_ref[...] = jnp.concatenate([big, big, low], axis=1).astype(BF16)
    inverse_ref[...] = inverse


def final_kernel(raw_ref, weights_ref, inverse_ref, merged_ref, out_ref, q_ref, hold_ref, q_buf, sem):
    here = lax.axis_index("shard")
    width = hold_ref.shape[1]
    step = raw_ref.shape[-1]
    gather = lambda peers: jnp.concatenate([raw_ref[core, peer] for core in range(2) for peer in peers], axis=0)
    peers = [here // 2 * 2 + 16 * z + k for z in range(2) for k in range(2)]
    raw = gather([jnp.where(peer == FIRST, 0, peer + (peer < FIRST).astype(jnp.int32)) for peer in peers])
    raw = jnp.where(here % 2 == 0, raw[:, : step // 2], raw[:, step // 2 :])
    q_buf[...] = dot(inverse_ref[...], raw, ((1,), (0,)), HIGH)
    copies = [pltpu.make_async_copy(q_buf, q_ref, sem.at[width // step])]
    copies[0].start()
    for g in range(width // step):
        cols = slice(g * step, (g + 1) * step)
        big, low = split(gather([place_of(16 * z + 2 * g + k) for z in range(2) for k in range(2)]), 2)
        approx = dot(weights_ref[...], jnp.concatenate([big, low, big], axis=0), ((1,), (0,)))
        hold_ref[:, cols] = merged_ref[:, cols] - approx
        copy = pltpu.make_async_copy(hold_ref.at[:, cols], out_ref.at[:, cols], sem.at[g])
        copy.start()
        copies.append(copy)
    for copy in copies:
        copy.wait()


def per_device(grads, errors, q_prev):
    shape = jax.ShapeDtypeStruct
    rows, width = errors.shape[1:]
    share, rank = q_prev.shape
    half = rank // 2
    replicas = 32

    (own_q,) = call(
        ask_kernel,
        [shape((16, half // 2, 2 * share), F32)],
        [q_prev.T],
        [VMEM],
    )
    all_q = exchange(own_q, "shard", order_of(16, ASKED))
    merged = grads[0].astype(F32) + errors[0]
    other = lax.ppermute(merged, "core", SWAP)
    (all_q,) = call(
        line_kernel,
        [shape((2 * half, width), BF16)],
        [all_q],
        [VMEM],
        flops=10**11,
    )
    parts, left = call(
        left_kernel,
        [shape((2 * rows, width), BF16), shape((16, 8, 128), F32)],
        [all_q, merged, other],
        [VMEM, VMEM, ANY],
        [pltpu.VMEM((rows, width), F32), pltpu.SemaphoreType.DMA((CUTS,))],
        flops=2 * 32 * 128 * width,
    )
    left = exchange(left, ("z8", "z0"), LEFT_Z)

    pieces, mine = call(
        functools.partial(right_kernel, replicas),
        [shape((32, half // 4, 1024), F32), shape((half, rows), F32)],
        [left, parts],
        [VMEM, VMEM],
        flops=2 * 32 * 128 * width,
    )
    pieces = exchange(pieces, PLANE, order_of(32))
    right, left_own = call(
        scatter_kernel,
        [shape((8, half // 4, 2 * share), F32), shape((half, 16 * rows), F32)],
        [pieces],
        [VMEM],
    )
    right = exchange(right, "z8", [z // 2 for z in RIGHT_Z])

    left_other = lax.ppermute(left_own, "core", SWAP)
    weights, inverse = call(
        factor_kernel,
        [shape((rows, 3 * rank), BF16), shape((rank, rank), F32)],
        [left_own, left_other, mine],
        [VMEM] * 3,
        [pltpu.VMEM((rank, 16 * rows), F32), pltpu.VMEM((rank, rows), F32)],
        flops=10**7,
    )

    (raw,) = call(
        spread_kernel, [shape((32, half // 4, 2 * share), F32)], [right, weights, inverse], [VMEM] * 3
    )
    raw = exchange(raw, PLANE, order_of(32))
    raw = lax.all_gather(raw, "core")
    out, q_new = call(
        final_kernel,
        [shape((rows, width), F32), shape((rank, share), F32)],
        [raw, weights, inverse, merged],
        [VMEM] * 4,
        [pltpu.VMEM((rows, width), F32), pltpu.VMEM((rank, share), F32), pltpu.SemaphoreType.DMA((9,))],
        [ANY, ANY],
        flops=2 * 96 * 64 * width,
    )
    return (out[None], q_new.T)


def solution(mesh):
    parts = Mesh(mesh.devices.reshape(8, 2, 2, 16), ("z8", "z0", "core", "shard"))
    dp = ("z8", "z0", "core")
    in_specs = (P(dp, "shard", None), P(dp, "shard", None), P("shard", None))
    out_specs = (P(dp, "shard", None), P("shard", None))
    return jax.shard_map(
        per_device, mesh=parts, in_specs=in_specs, out_specs=out_specs, check_vma=False
    )
```
